256 devices in a mesh: grp: 8 (over z), dom: 32 (over x, y, core).
Axes of the slice: x: 4, y: 4, z: 8, core: 2. Of those that a mesh axis runs over, the one named last changes fastest.
Arguments:
- hidden_in: bfloat16 [524288, 128], P(('grp', 'dom')), may hold values from -6 to 6
- cotangent: bfloat16 [524288, 128], P(('grp', 'dom')), may hold values from -6 to 6
- coarse_state: bfloat16 [32768, 128], P(('grp', 'dom')), may hold values from -6 to 6
- edge_self: bfloat16 [128, 128], replicated, may hold values from -0.375 to 0.375
- edge_peer: bfloat16 [128, 128], replicated, may hold values from -0.375 to 0.375
- edge_out: bfloat16 [128, 128], replicated, may hold values from -0.1875 to 0.1875
- coarse_self: bfloat16 [128, 128], replicated, may hold values from -0.375 to 0.375
- coarse_peer: bfloat16 [128, 128], replicated, may hold values from -0.375 to 0.375
- coarse_out: bfloat16 [128, 128], replicated, may hold values from -0.1875 to 0.1875
- fine_nbrs: int32 [524288, 8], P(('grp', 'dom')), may hold values from 0 to 2304, as said below
- rim_rows: int32 [65536], P(('grp', 'dom')), may hold values from 0 to 2047, as said below
- send_lists: int32 [8192, 128], P(('grp', 'dom')), may hold values from 0 to 2048, as said below
- member_slots: int32 [8192, 128], P(('grp', 'dom')), may hold values from 0 to 128, as said below
- own_slots: int32 [524288], P(('grp', 'dom')), may hold values from 0 to 128, as said below
- coarse_nbrs: int32 [32768, 8], P(('grp', 'dom')), may hold values from 0 to 128
Outputs:
- hidden_grad: float32 [524288, 128], P(('grp', 'dom'))
- grad_edge_self: float32 [128, 128], replicated
- grad_edge_peer: float32 [128, 128], replicated
- grad_edge_out: float32 [128, 128], replicated
- grad_coarse_self: float32 [128, 128], replicated
- grad_coarse_peer: float32 [128, 128], replicated
- grad_coarse_out: float32 [128, 128], replicated
The draws below stay inside these ranges and needn't reach their ends.
Inputs may be any that keep to these rules, and one draw needn't show every extreme that they name: `fine_nbrs`: each entry of a fine node's list is a local row of the node's own aligned block of min(512, 2048) rows, a rim row (2048 to 2303), or 2304 for an empty slot. `rim_rows`: distinct local fine rows of the subdomain; the first 128 go to the lower adjacent subdomain, the last 128 to the upper one. `send_lists`: entry 2048 marks an empty slot and fills the tail of each list. A subdomain sends rows only to owners at most two positions away in its group and to the owner 32 // 2 positions away counted round, never to itself; every fine node is sent at most once. Each subdomain sends at most 128 rows to one owner and exactly 128 to one of its adjacent owners. member_slots[o, s, q] is the coarse node of owner o that row send_lists[s, o, q] joins, and 128 exactly where that row is 2048. `own_slots`: 128 exactly for the fine nodes that the subdomain sends away; every coarse node has at least one kept fine node of its own subdomain.
All inputs are finite; a program needn't handle non-finite values.
Results may differ from the reference program's by a relative error of at most 0.007.
Values may be sent and summed in bfloat16 or wider, within the bound.
A program may use at most 64 MiB of HBM per device.

```python
import jax
import jax.numpy as jnp
from jax import lax

LATENT = 128
SLOTS = 8
CSLOTS = 8
FINE_DEV = 2048
COARSE_DEV = 128
RIM = 128
SENDS = 128
NODES = 524288
COARSE = 32768
N_GRP = 8
N_DOM = 32


def one_order(small_key):
    return jax.random.permutation(small_key, FINE_DEV)


def owner_offsets():
    return (-2, -1, 1, 2, N_DOM // 2)


def route_tables(key):
    devices = N_GRP * N_DOM
    side = jnp.arange(devices, dtype=jnp.int32) % N_DOM
    count_key, order_key, slot_key, own_key = jax.random.split(key, 4)
    near = jnp.array([-2, -1, 1, 2], dtype=jnp.int32)
    near_targets = side[:, None] + near[None, :]
    far_target = ((side + N_DOM // 2) % N_DOM)[:, None]
    targets = jnp.concatenate([near_targets, far_target], axis=1).astype(jnp.int32)
    exists = (targets >= 0) & (targets < N_DOM)
    counts = jax.random.randint(count_key, (devices, 5), SENDS // 2, SENDS + 1).astype(jnp.int32)
    forced = jnp.where(side < N_DOM - 1, 2, 1)
    columns = jnp.arange(5, dtype=jnp.int32)
    counts = jnp.where(columns[None, :] == forced[:, None], SENDS, counts)
    counts = jnp.where(exists, counts, 0).astype(jnp.int32)
    ends = jnp.cumsum(counts, axis=1).astype(jnp.int32)
    starts = ends - counts
    leaving = ends[:, 4]
    orders = jax.vmap(one_order)(jax.random.split(order_key, devices)).astype(jnp.int32)
    places = jnp.arange(SENDS, dtype=jnp.int32)
    wanted = jnp.minimum(starts[:, :, None] + places[None, None, :], FINE_DEV - 1).reshape(devices, 5 * SENDS)
    chosen = jnp.take_along_axis(orders, wanted, axis=1).reshape(devices, 5, SENDS)
    filled = places[None, None, :] < counts[:, :, None]
    sent = jnp.where(filled, chosen, FINE_DEV).astype(jnp.int32)
    far_slots = jnp.where(filled, jax.random.randint(slot_key, (devices, 5, SENDS), 0, COARSE_DEV), COARSE_DEV).astype(jnp.int32)
    ranks = jnp.argsort(orders, axis=1).astype(jnp.int32)
    kept_rank = ranks - leaving[:, None]
    spread = jax.random.randint(own_key, (devices, FINE_DEV), 0, COARSE_DEV).astype(jnp.int32)
    owned = jnp.where(kept_rank < COARSE_DEV, kept_rank, spread)
    owned = jnp.where(kept_rank >= 0, owned, COARSE_DEV).astype(jnp.int32)
    return (targets, sent, far_slots, owned)


def draw_send_lists(key, part):
    targets, sent, far_slots, owned = route_tables(key)
    devices = N_GRP * N_DOM
    peers = jnp.arange(N_DOM, dtype=jnp.int32)
    table = jnp.full((devices, N_DOM, SENDS), FINE_DEV, dtype=jnp.int32)
    for column in range(5):
        matched = (peers[None, :] == targets[:, column:column + 1])[:, :, None]
        table = jnp.where(matched, sent[:, column][:, None, :], table)
    return table.reshape(devices * N_DOM, SENDS)


def draw_member_slots(key, part):
    targets, sent, far_slots, owned = route_tables(key)
    grouped = far_slots.reshape(N_GRP, N_DOM, 5, SENDS)
    owners = jnp.arange(N_DOM, dtype=jnp.int32)[:, None]
    sources = jnp.arange(N_DOM, dtype=jnp.int32)[None, :]
    table = jnp.full((N_GRP, N_DOM, N_DOM, SENDS), COARSE_DEV, dtype=jnp.int32)
    for column, shift_by in enumerate(owner_offsets()):
        moved = jnp.roll(grouped[:, :, column], shift_by, axis=1)
        matched = (sources == (owners - shift_by) % N_DOM)[None, :, :, None]
        table = jnp.where(matched, moved[:, :, None, :], table)
    return table.reshape(N_GRP * N_DOM * N_DOM, SENDS)


def draw_own_slots(key, part):
    targets, sent, far_slots, owned = route_tables(key)
    return owned.reshape(-1)


def draw_rim_rows(key, part):
    key = jax.random.fold_in(key, 5)
    devices = N_GRP * N_DOM
    orders = jax.vmap(one_order)(jax.random.split(key, devices)).astype(jnp.int32)
    return orders[:, :2 * RIM].reshape(-1)


def draw_fine_nbrs(key, part):
    key = jax.random.fold_in(key, 19)
    kind_key, own_key, rim_key = jax.random.split(key, 3)
    block = min(512, FINE_DEV)
    local = jnp.arange(NODES, dtype=jnp.int32) % FINE_DEV
    base = local // block * block
    kinds = jax.random.randint(kind_key, (NODES, SLOTS), 0, 10)
    inside = base[:, None] + jax.random.randint(own_key, (NODES, SLOTS), 0, block)
    rimmed = FINE_DEV + jax.random.randint(rim_key, (NODES, SLOTS), 0, 2 * RIM)
    chosen = jnp.where(kinds < 6, inside, jnp.where(kinds < 9, rimmed, FINE_DEV + 2 * RIM))
    return chosen.astype(jnp.int32)


def plant(drawn, stream_key, smallest, top_value):
    longest = drawn.shape.index(max(drawn.shape))
    spots = []
    for shift in (0, 1):
        where = [jax.random.randint(jax.random.fold_in(stream_key, axis), (), 0, length) for axis, length in enumerate(drawn.shape)]
        where[longest] = (where[longest] + shift) % drawn.shape[longest]
        spots.append(tuple(where))
    return drawn.at[spots[0]].set(smallest).at[spots[1]].set(top_value)


def steps_of(key, extent, cuts, low, top_value):
    def one(dim, blocks):
        steps = jax.random.uniform(jax.random.fold_in(jax.random.fold_in(key, 6), dim), (blocks,), jnp.float32, low / len(cuts), top_value / len(cuts))
        return jnp.repeat(jnp.exp(steps), extent[dim] // blocks).reshape((-1,) + (1,) * (len(extent) - dim - 1))

    factor_of = one(*cuts[0])
    for cut in cuts[1:]:
        factor_of = factor_of * one(*cut)
    return factor_of


def noise(key, extent, scale, reach, pieces=(), held_as=jnp.bfloat16):
    factor_of = steps_of(key, extent, pieces, -0.22, 0.18) if pieces else 1.0
    entries = jax.random.normal(key, extent, jnp.float32) * scale * factor_of
    return jnp.minimum(jnp.maximum(entries, -reach), reach).astype(held_as)


def setup_inputs(seed: int = 0) -> dict:
    seeds = jax.random.split(jax.random.key(seed), 16)
    return {
        "hidden_in": noise(seeds[0], (NODES, LATENT), 1.0, 6.0, ((0, 256),)),
        "cotangent": noise(seeds[1], (NODES, LATENT), 1.0, 6.0, ((0, 256),)),
        "coarse_state": noise(seeds[2], (COARSE, LATENT), 1.0, 6.0, ((0, 256),)),
        "edge_self": noise(seeds[3], (LATENT, LATENT), (2 * LATENT) ** -0.5, 0.375),
        "edge_peer": noise(seeds[4], (LATENT, LATENT), (2 * LATENT) ** -0.5, 0.375),
        "edge_out": noise(seeds[5], (LATENT, LATENT), (SLOTS * LATENT) ** -0.5, 0.1875),
        "coarse_self": noise(seeds[6], (LATENT, LATENT), (2 * LATENT) ** -0.5, 0.375),
        "coarse_peer": noise(seeds[7], (LATENT, LATENT), (2 * LATENT) ** -0.5, 0.375),
        "coarse_out": noise(seeds[8], (LATENT, LATENT), (CSLOTS * LATENT) ** -0.5, 0.1875),
        "fine_nbrs": draw_fine_nbrs(jax.random.fold_in(seeds[15], 71), 0),
        "rim_rows": draw_rim_rows(jax.random.fold_in(seeds[15], 71), 0),
        "send_lists": draw_send_lists(jax.random.fold_in(seeds[15], 71), 0),
        "member_slots": draw_member_slots(jax.random.fold_in(seeds[15], 71), 0),
        "own_slots": draw_own_slots(jax.random.fold_in(seeds[15], 71), 0),
        "coarse_nbrs": plant(jax.random.randint(seeds[14], (COARSE, CSLOTS), 0, COARSE_DEV + 1), jax.random.fold_in(seeds[14], 1), 0, COARSE_DEV).astype(jnp.int32),
    }


def inner_product(left_rows, right_rows):
    return lax.dot_general(left_rows, right_rows, (((0,), (0,)), ((), ())), preferred_element_type=jnp.float32)


def times_transpose(values, weight):
    return lax.dot_general(values, weight, (((1,), (1,)), ((), ())), preferred_element_type=jnp.float32)


def exact_transpose(values, weight):
    return lax.dot_general(values, weight.astype(jnp.float32), (((1,), (1,)), ((), ())), precision=lax.Precision.HIGHEST, preferred_element_type=jnp.float32)


def message_backward(lookup, upstream, neighbors, weight_self, weight_peer, weight_out):
    node_count, slot_count = neighbors.shape
    latent_width = lookup.shape[1]
    pad_row = lookup.shape[0] - 1
    block_rows = min(512, node_count)
    block_count = node_count // block_rows

    def one_block(carried, block_number):
        peer_sum, self_grad, grad_self, grad_peer, grad_out = carried
        first_row = block_number * block_rows
        selves = lax.dynamic_slice_in_dim(lookup, first_row, block_rows, 0)
        picked = lax.dynamic_slice_in_dim(neighbors, first_row, block_rows, 0)
        peer_rows = lookup[picked].reshape(block_rows * slot_count, latent_width)
        usable = (picked < pad_row).astype(jnp.float32)[:, :, None]
        pre_self = jnp.dot(selves, weight_self, preferred_element_type=jnp.float32)
        pre_peer = jnp.dot(peer_rows, weight_peer, preferred_element_type=jnp.float32).reshape(block_rows, slot_count, latent_width)
        summed = pre_self[:, None, :] + pre_peer
        squash = jax.nn.sigmoid(summed)
        pooled = jnp.sum(usable * summed * squash, axis=1).astype(jnp.bfloat16)
        arriving = lax.dynamic_slice_in_dim(upstream, first_row, block_rows, 0)
        arriving_b = arriving.astype(jnp.bfloat16)
        grad_out = grad_out + inner_product(pooled, arriving_b)
        grad_pooled = times_transpose(arriving_b, weight_out)
        grad_pre = usable * grad_pooled[:, None, :] * squash * (1.0 + summed * (1.0 - squash))
        grad_pre_b = grad_pre.astype(jnp.bfloat16).reshape(block_rows * slot_count, latent_width)
        grad_sum_b = jnp.sum(grad_pre, axis=1).astype(jnp.bfloat16)
        grad_self = grad_self + inner_product(selves, grad_sum_b)
        grad_peer = grad_peer + inner_product(peer_rows, grad_pre_b)
        to_self = arriving + times_transpose(grad_sum_b, weight_self)
        peer_sum = peer_sum.at[picked.reshape(-1)].add(grad_pre_b.astype(jnp.float32))
        self_grad = lax.dynamic_update_slice_in_dim(self_grad, to_self, first_row, 0)
        return (peer_sum, self_grad, grad_self, grad_peer, grad_out), None

    square = jnp.zeros((latent_width, latent_width), jnp.float32)
    initial = (jnp.zeros((lookup.shape[0], latent_width), jnp.float32), jnp.zeros((node_count, latent_width), jnp.float32), square, square, square)
    finished, unused = lax.scan(one_block, initial, jnp.arange(block_count, dtype=jnp.int32))
    peer_sum, self_grad, grad_self, grad_peer, grad_out = finished
    table_grad = exact_transpose(peer_sum[:pad_row], weight_peer)
    return self_grad + table_grad[:node_count], table_grad[node_count:], (grad_self, grad_peer, grad_out)


def far_sum(member_list, arrived, slot_count):
    slot_ids = jnp.arange(slot_count, dtype=jnp.int32)[:, None]
    matches = (member_list.reshape(1, -1) == slot_ids).astype(jnp.bfloat16)
    return jnp.dot(matches, arrived.reshape(-1, arrived.shape[-1]), preferred_element_type=jnp.float32)


def owner_work(local_cot, own_list, member_list, grad_far, coarse_rows, coarse_links, weight_self, weight_peer, weight_out):
    slot_count, latent_width = coarse_rows.shape
    slot_ids = jnp.arange(slot_count, dtype=jnp.int32)[:, None]
    own_match = own_list[None, :] == slot_ids
    far_match = member_list.reshape(1, -1) == slot_ids
    pulled = jnp.dot(own_match.astype(jnp.bfloat16), local_cot, preferred_element_type=jnp.float32) + grad_far
    members = (jnp.sum(own_match.astype(jnp.int32), axis=1) + jnp.sum(far_match.astype(jnp.int32), axis=1)).astype(jnp.float32)
    zero_row = jnp.zeros((1, latent_width), jnp.bfloat16)
    lookup = jnp.concatenate([coarse_rows, zero_row], axis=0)
    node_grad, unused, grads = message_backward(lookup, pulled, coarse_links, weight_self, weight_peer, weight_out)
    back_rows = (node_grad / members[:, None]).astype(jnp.bfloat16)
    return jnp.concatenate([back_rows, zero_row], axis=0), grads


def fine_grad_in(local_cot, back_rows, own_list, send_list, replies):
    latent_width = local_cot.shape[1]
    upstream = local_cot.astype(jnp.float32) + back_rows[own_list].astype(jnp.float32)
    padded = jnp.concatenate([upstream, jnp.zeros((1, latent_width), jnp.float32)], axis=0)
    padded = padded.at[send_list.reshape(-1)].add(replies.reshape(-1, latent_width).astype(jnp.float32))
    return padded[:-1]


def reference(hidden_in, cotangent, coarse_state, edge_self, edge_peer, edge_out, coarse_self, coarse_peer, coarse_out, fine_nbrs, rim_rows, send_lists, member_slots, own_slots, coarse_nbrs):
    devices = N_GRP * N_DOM
    hidden_blocks = hidden_in.reshape(N_GRP, N_DOM, FINE_DEV, LATENT)
    cot_blocks = cotangent.reshape(N_GRP, N_DOM, FINE_DEV, LATENT)
    cot_padded = jnp.concatenate([cot_blocks, jnp.zeros((N_GRP, N_DOM, 1, LATENT), jnp.bfloat16)], axis=2)
    sends = send_lists.reshape(N_GRP, N_DOM, N_DOM, SENDS)
    members = member_slots.reshape(N_GRP, N_DOM, N_DOM, SENDS)
    owns = own_slots.reshape(devices, FINE_DEV)
    links = fine_nbrs.reshape(devices, FINE_DEV, SLOTS)
    rims = rim_rows.reshape(N_GRP, N_DOM, 2 * RIM)
    coarse_blocks = coarse_state.reshape(devices, COARSE_DEV, LATENT)
    coarse_links = coarse_nbrs.reshape(devices, COARSE_DEV, CSLOTS)
    sources = jnp.arange(N_DOM, dtype=jnp.int32)[:, None]

    def owner_step(device):
        group = device // N_DOM
        side = device % N_DOM
        arrived = cot_padded[group][sources, sends[group, :, side, :]]
        grad_far = far_sum(members[group, side], arrived, COARSE_DEV)
        return owner_work(cot_blocks[group, side], owns[device], members[group, side], grad_far, coarse_blocks[device], coarse_links[device], coarse_self, coarse_peer, coarse_out)

    back_all, coarse_grads = lax.map(owner_step, jnp.arange(devices, dtype=jnp.int32))
    back_all = back_all.reshape(N_GRP, N_DOM, COARSE_DEV + 1, LATENT)
    zero_rim = jnp.zeros((RIM, LATENT), jnp.bfloat16)
    zero_row = jnp.zeros((1, LATENT), jnp.bfloat16)

    def fine_step(device):
        group = device // N_DOM
        side = device % N_DOM
        replies = back_all[group][sources, members[group, :, side, :]]
        upstream = fine_grad_in(cot_blocks[group, side], back_all[group, side], owns[device], sends[group, side], replies)
        lower = jnp.maximum(side - 1, 0)
        upper = jnp.minimum(side + 1, N_DOM - 1)
        from_lower = jnp.where(side > 0, hidden_blocks[group, lower][rims[group, lower, RIM:]], zero_rim)
        from_upper = jnp.where(side < N_DOM - 1, hidden_blocks[group, upper][rims[group, upper, :RIM]], zero_rim)
        lookup = jnp.concatenate([hidden_blocks[group, side], from_lower, from_upper, zero_row], axis=0)
        return message_backward(lookup, upstream, links[device], edge_self, edge_peer, edge_out)

    node_grads, rim_grads, fine_grads = lax.map(fine_step, jnp.arange(devices, dtype=jnp.int32))
    rim_all = rim_grads.reshape(N_GRP, N_DOM, 2 * RIM, LATENT)
    zero_block = jnp.zeros((N_GRP, 1, RIM, LATENT), jnp.float32)
    lower_parts = jnp.concatenate([zero_block, rim_all[:, :-1, RIM:]], axis=1).reshape(devices, RIM, LATENT)
    upper_parts = jnp.concatenate([rim_all[:, 1:, :RIM], zero_block], axis=1).reshape(devices, RIM, LATENT)
    flat_rims = rims.reshape(devices, 2 * RIM)

    def add_rims(node_grad, rim_list, lower_part, upper_part):
        return node_grad.at[rim_list[:RIM]].add(lower_part).at[rim_list[RIM:]].add(upper_part)

    hidden_grad = jax.vmap(add_rims)(node_grads, flat_rims, lower_parts, upper_parts).reshape(NODES, LATENT)
    return (hidden_grad, jnp.sum(fine_grads[0], axis=0), jnp.sum(fine_grads[1], axis=0), jnp.sum(fine_grads[2], axis=0), jnp.sum(coarse_grads[0], axis=0), jnp.sum(coarse_grads[1], axis=0), jnp.sum(coarse_grads[2], axis=0))
```

```python
import functools

import jax
import jax.numpy as jnp
from jax import lax
from jax.experimental import pallas as pl
from jax.experimental.pallas import tpu as pltpu
from jax.sharding import PartitionSpec as P

MESH = pl.DeviceIdType.MESH
F32 = jnp.float32
BF16 = jnp.bfloat16
OFF = -1.0e4


def dot(a, b):
    return jnp.dot(a, b, preferred_element_type=F32)


def dot_nt(a, b):
    return lax.dot_general(a, b, (((1,), (1,)), ((), ())), preferred_element_type=F32)


def dot_tn(a, b):
    return lax.dot_general(a, b, (((0,), (0,)), ((), ())), preferred_element_type=F32)


def one_hot(index, shape, axis):
    ids = lax.broadcasted_iota(jnp.int32, shape, axis).astype(jnp.int16)
    hit = jnp.broadcast_to(index.astype(jnp.int16), shape) == ids
    return jnp.where(hit, jnp.ones(shape, BF16), jnp.zeros(shape, BF16))


def in_columns(index, width):
    return one_hot(index, (index.shape[0], width), 1)


def in_rows(index, height):
    return one_hot(index, (height, index.shape[1]), 0)


def split(values):
    high = values.astype(BF16)
    return high, (values - high.astype(F32)).astype(BF16)


def gate(pre):
    squash = 0.5 + 0.5 * jnp.tanh(0.5 * pre)
    act = pre * squash
    return act, squash + act * (1.0 - squash)


def block_kernel(
    n_dom,
    hidden_ref,
    cot_ref,
    coarse_ref,
    ws_ref,
    wp_ref,
    wo_ref,
    cws_ref,
    cwp_ref,
    cwo_ref,
    nbrs_ref,
    rim_ref,
    send_ref,
    member_ref,
    own_ref,
    cnbrs_ref,
    out_ref,
    grads_ref,
    cot_out,
    cot_in,
    rep_out,
    rep_in,
    rim_out,
    rim_in,
    ret_out,
    ret_in,
    peer_hl,
    pre_self_ref,
    window,
    slope_ref,
    pooled_ref,
    own_cols,
    place_ref,
    rim_sum,
    send_sem,
    recv_sem,
):
    grp = lax.axis_index("grp")
    me = lax.axis_index("dom")
    fine, width = hidden_ref.shape
    coarse = coarse_ref.shape[0]
    slots = nbrs_ref.shape[0]
    rim = rim_ref.shape[1]
    sends = send_ref.shape[1]
    block = min(512, fine)
    blocks = fine // block
    span = block + 2 * rim
    offsets = (1, -1, 2, -2, n_dom // 2)
    to = [lax.rem(me + (n_dom + o), n_dom) for o in offsets]
    source = [lax.rem(me + (n_dom - o), n_dom) for o in offsets]

    barrier = pltpu.get_barrier_semaphore()
    for peer in to:
        pl.semaphore_signal(barrier, inc=1, device_id=(grp, peer), device_id_type=MESH)

    def remote(src, dst, index, peer):
        return pltpu.make_async_remote_copy(
            src_ref=src,
            dst_ref=dst,
            send_sem=send_sem.at[index],
            recv_sem=recv_sem.at[index],
            device_id=(grp, peer),
            device_id_type=MESH,
        )

    cot_copies = [remote(cot_out.at[k], cot_in.at[k], k, to[k]) for k in range(5)]
    rim_copies = [remote(rim_out.at[k], rim_in.at[k], 5 + k, to[k]) for k in range(2)]
    rep_copies = [remote(rep_out.at[k], rep_in.at[k], 7 + k, source[k]) for k in range(5)]
    ret_copies = [remote(ret_out.at[k], ret_in.at[k], 12 + k, to[k]) for k in range(2)]

    send_rows = [send_ref[pl.ds(t, 1), :] for t in to]
    member_rows = [member_ref[pl.ds(s, 1), :] for s in source]
    listed = jnp.concatenate(
        send_rows + [rim_ref[1:2, :], rim_ref[0:1, :], jnp.zeros((1, sends), jnp.int32)], axis=0
    )
    listed_cols = listed.T
    for k in range(5):
        cot_out[k] = dot(in_columns(listed_cols[:, k : k + 1], fine), cot_ref[...]).astype(BF16)
    pl.semaphore_wait(barrier, 5)
    for copy in cot_copies:
        copy.start()
    for k in range(2):
        rim_out[k] = dot(in_columns(listed_cols[:, 5 + k : 6 + k], fine), hidden_ref[...]).astype(
            BF16
        )
    for copy in rim_copies:
        copy.start()

    own_cols[...] = own_ref[...].T
    own_hot = jnp.concatenate(
        [in_rows(own_ref[t : t + 1, :], coarse) for t in range(fine // 128)], axis=1
    )
    far_hot = jnp.concatenate([in_rows(row, coarse) for row in member_rows], axis=1)
    own_pull = dot(own_hot, cot_ref[...])
    members = dot(own_hot, jnp.ones((fine, width), BF16)) + dot(
        far_hot, jnp.ones((5 * sends, width), BF16)
    )

    coarse_rows = coarse_ref[...]
    coarse_self = dot(coarse_rows, cws_ref[...])
    coarse_peer = jnp.concatenate(split(dot(coarse_rows, cwp_ref[...])), axis=1)
    links = cnbrs_ref[...]
    link_cols = links.T
    coarse_slopes = []
    coarse_pool = jnp.zeros((coarse, width), F32)
    for j in range(slots):
        col = link_cols[:, j : j + 1]
        got = dot(in_columns(col, coarse), coarse_peer)
        bias = jnp.where(col == coarse, OFF, 0.0)
        act, slope = gate(coarse_self + got[:, :width] + (got[:, width:] + bias))
        coarse_pool += act
        coarse_slopes.append(slope)
    coarse_pool = coarse_pool.astype(BF16)

    both = dot(hidden_ref[...], jnp.concatenate([ws_ref[...], wp_ref[...]], axis=1))
    pre_self_ref[...] = both[:, :width]
    high, low = split(both[:, width:])
    peer_hl[0:fine, 0:width] = high
    peer_hl[0:fine, width:] = low

    for copy in cot_copies:
        copy.wait()
    far_pull = dot(far_hot, cot_in[...].reshape(5 * sends, width))
    pulled = own_pull + far_pull
    pulled_b = pulled.astype(BF16)
    grad_pool = dot_nt(pulled_b, cwo_ref[...])
    grad_sum = jnp.zeros((coarse, width), F32)
    peer_sum = jnp.zeros((coarse, width), F32)
    for j in range(slots):
        grad_pre = grad_pool * coarse_slopes[j]
        grad_sum += grad_pre
        peer_sum += dot(in_rows(links[j : j + 1, :], coarse), grad_pre.astype(BF16))
    grad_sum = grad_sum.astype(BF16)
    high, low = split(peer_sum)
    node_grad = pulled + dot_nt(grad_sum, cws_ref[...])
    node_grad += dot_nt(high, cwp_ref[...]) + dot_nt(low, cwp_ref[...])
    back = (node_grad / members).astype(BF16)
    member_cols = jnp.concatenate(
        member_rows + [jnp.zeros((3, sends), jnp.int32)], axis=0
    ).T
    for k in range(5):
        rep_out[k] = dot(in_columns(member_cols[:, k : k + 1], coarse), back).astype(BF16)
    for copy in rep_copies:
        copy.start()
    grads_ref[3 * width : 4 * width, :] = dot_tn(coarse_rows, grad_sum)
    grads_ref[4 * width : 5 * width, :] = dot_tn(coarse_rows, high) + dot_tn(coarse_rows, low)
    grads_ref[5 * width : 6 * width, :] = dot_tn(coarse_pool, pulled_b)

    for copy in rim_copies:
        copy.wait()
    lower = jnp.where(me > 0, 1.0, 0.0).astype(BF16)
    upper = jnp.where(me < n_dom - 1, 1.0, 0.0).astype(BF16)
    rims = jnp.concatenate([rim_in[0] * lower, rim_in[1] * upper], axis=0)
    high, low = split(dot(rims, wp_ref[...]))
    window[block:, 0:width] = high
    window[block:, width:] = low

    def forward(b, carry):
        first = pl.multiple_of(b * block, block)
        here = pl.ds(first, block)
        picked = nbrs_ref[:, here]
        placed = jnp.where(picked < fine, picked - first, picked - fine + block)
        place_ref[b] = placed
        cols = placed.T
        window[0:block, :] = peer_hl[here, :]
        own_pre = pre_self_ref[here, :]
        total = jnp.zeros((block, width), F32)
        for j in range(slots):
            col = cols[:, j : j + 1]
            got = dot(in_columns(col, span), window[...])
            bias = jnp.where(col == span, OFF, 0.0)
            act, slope = gate(own_pre + got[:, :width] + (got[:, width:] + bias))
            total += act
            slope_ref[b, j] = slope
        pooled_ref[here, :] = total.astype(BF16)
        return carry

    lax.fori_loop(0, blocks, forward, 0)

    for copy in rep_copies:
        copy.wait()
    sources = jnp.concatenate([back, rep_in[...].reshape(5 * sends, width)], axis=0)
    grads_ref[0 : 3 * width, :] = jnp.zeros((3 * width, width), F32)
    rim_sum[...] = jnp.zeros((2 * rim, width), F32)
    self_weight = ws_ref[...]
    peer_weight = wp_ref[...]
    out_weight = wo_ref[...]

    def backward(b, carry):
        first = pl.multiple_of(b * block, block)
        here = pl.ds(first, block)
        own_hots = jnp.concatenate(
            [
                in_columns(own_ref[pl.ds(b * (block // 128) + t, 1), :].T, coarse)
                for t in range(block // 128)
            ],
            axis=0,
        )
        hots = jnp.concatenate([own_hots] + [in_rows(row - first, block) for row in send_rows], axis=1)
        arriving = cot_ref[here, :].astype(F32) + dot(hots, sources)
        arriving_b = arriving.astype(BF16)
        grad_pool = dot_nt(arriving_b, out_weight)
        grad_sum = jnp.zeros((block, width), F32)
        peer_sum = jnp.zeros((span, width), F32)
        placed = place_ref[b]
        for j in range(slots):
            grad_pre = grad_pool * slope_ref[b, j]
            grad_sum += grad_pre
            peer_sum += dot(in_rows(placed[j : j + 1, :], span), grad_pre.astype(BF16))
        grad_sum = grad_sum.astype(BF16)
        rim_sum[...] += peer_sum[block:]
        high, low = split(peer_sum[:block])
        rows = hidden_ref[here, :]
        got = dot_tn(rows, jnp.concatenate([grad_sum, high, low], axis=1))
        grads_ref[0:width, :] += got[:, :width]
        grads_ref[width : 2 * width, :] += got[:, width : 2 * width] + got[:, 2 * width :]
        grads_ref[2 * width : 3 * width, :] += dot_tn(pooled_ref[here, :], arriving_b)
        out_ref[here, :] = (
            arriving
            + dot_nt(grad_sum, self_weight)
            + dot_nt(high, peer_weight)
            + dot_nt(low, peer_weight)
        )
        return carry

    lax.fori_loop(0, blocks, backward, 0)

    high, low = split(rim_sum[...])
    rim_grad = (dot_nt(high, peer_weight) + dot_nt(low, peer_weight)).astype(BF16)
    ret_out[0] = rim_grad[rim:]
    ret_out[1] = rim_grad[:rim]
    for copy in ret_copies:
        copy.start()
    grads_ref[width : 2 * width, :] += dot_tn(rims, high) + dot_tn(rims, low)
    for copy in ret_copies:
        copy.wait()
    returned = jnp.concatenate([ret_in[0] * lower, ret_in[1] * upper], axis=0)

    def give_back(b, carry):
        first = pl.multiple_of(b * block, block)
        here = pl.ds(first, block)
        hots = jnp.concatenate([in_rows(rim_ref[k : k + 1, :] - first, block) for k in range(2)], axis=1)
        out_ref[here, :] += dot(hots, returned)
        return carry

    lax.fori_loop(0, blocks, give_back, 0)


def sum_kernel(n_grp, n_dom, part_ref, out_ref, first_in, mine, second_in, send_sem, recv_sem):
    grp = lax.axis_index("grp")
    dom = lax.axis_index("dom")
    plane = n_dom // 2
    column = n_grp * 2
    core = lax.rem(dom, 2)
    place = dom // 2
    level = grp * 2 + core
    rows = part_ref.shape[0] // plane

    def in_plane(index):
        return (grp, index * 2 + core)

    def in_column(index):
        return (index // 2, place * 2 + lax.rem(index, 2))

    barrier = pltpu.get_barrier_semaphore()
    for t in range(1, plane):
        pl.semaphore_signal(
            barrier, inc=1, device_id=in_plane(lax.rem(place + t, plane)), device_id_type=MESH
        )
    for t in range(1, column):
        pl.semaphore_signal(
            barrier, inc=1, device_id=in_column(lax.rem(level + t, column)), device_id_type=MESH
        )
    pl.semaphore_wait(barrier, plane + column - 2)

    def cut(index):
        return pl.ds(pl.multiple_of(index * rows, 8), rows)

    def copy(src, dst, index, peer):
        return pltpu.make_async_remote_copy(
            src_ref=src,
            dst_ref=dst,
            send_sem=send_sem.at[index],
            recv_sem=recv_sem.at[index],
            device_id=peer,
            device_id_type=MESH,
        )

    def ahead(t):
        return lax.rem(place + t, plane)

    first = [
        copy(part_ref.at[cut(ahead(t)), :], first_in.at[place], t, in_plane(ahead(t)))
        for t in range(1, plane)
    ]
    for c in first:
        c.start()
    first_in[place] = part_ref[cut(place), :]
    for c in first:
        c.wait()
    total = first_in[0]
    for t in range(1, plane):
        total += first_in[t]
    mine[...] = total
    second = [
        copy(mine, second_in.at[level], plane + t, in_column(lax.rem(level + t, column)))
        for t in range(1, column)
    ]
    for c in second:
        c.start()
    second_in[level] = total
    for c in second:
        c.wait()
    total = second_in[0]
    for t in range(1, column):
        total += second_in[t]
    out_ref[cut(place), :] = total
    third = [
        copy(
            out_ref.at[cut(place), :],
            out_ref.at[cut(place), :],
            plane + column + t,
            in_plane(ahead(t)),
        )
        for t in range(1, plane)
    ]
    for c in third:
        c.start()
    for c in third:
        c.wait()


def finish_kernel(node_ref, sums_ref, out_ref, *rest):
    parts, sem = rest[:-1], rest[-1]
    width = sums_ref.shape[1]
    copies = [pltpu.make_async_copy(node_ref, out_ref, sem.at[6])]
    for k, part in enumerate(parts):
        copies.append(
            pltpu.make_async_copy(sums_ref.at[pl.ds(k * width, width), :], part, sem.at[k])
        )
    for copy in copies:
        copy.start()
    for copy in copies:
        copy.wait()


def body(
    n_grp,
    n_dom,
    hidden_in,
    cotangent,
    coarse_state,
    edge_self,
    edge_peer,
    edge_out,
    coarse_self,
    coarse_peer,
    coarse_out,
    fine_nbrs,
    rim_rows,
    send_lists,
    member_slots,
    own_slots,
    coarse_nbrs,
):
    fine, width = hidden_in.shape
    coarse = coarse_state.shape[0]
    slots = fine_nbrs.shape[1]
    rim = rim_rows.shape[0] // 2
    sends = send_lists.shape[1]
    block = min(512, fine)
    blocks = fine // block
    vmem = pl.BlockSpec(memory_space=pltpu.VMEM)
    node_grad, grads = pl.pallas_call(
        functools.partial(block_kernel, n_dom),
        out_shape=(
            jax.ShapeDtypeStruct((fine, width), F32),
            jax.ShapeDtypeStruct((6 * width, width), F32),
        ),
        in_specs=[vmem] * 15,
        out_specs=(vmem, vmem),
        scratch_shapes=[
            pltpu.VMEM((5, sends, width), BF16),
            pltpu.VMEM((5, sends, width), BF16),
            pltpu.VMEM((5, sends, width), BF16),
            pltpu.VMEM((5, sends, width), BF16),
            pltpu.VMEM((2, rim, width), BF16),
            pltpu.VMEM((2, rim, width), BF16),
            pltpu.VMEM((2, rim, width), BF16),
            pltpu.VMEM((2, rim, width), BF16),
            pltpu.VMEM((fine, 2 * width), BF16),
            pltpu.VMEM((fine, width), F32),
            pltpu.VMEM((block + 2 * rim, 2 * width), BF16),
            pltpu.VMEM((blocks, slots, block, width), F32),
            pltpu.VMEM((fine, width), BF16),
            pltpu.VMEM((128, fine // 128), jnp.int32),
            pltpu.VMEM((blocks, slots, block), jnp.int32),
            pltpu.VMEM((2 * rim, width), F32),
            pltpu.SemaphoreType.DMA((14,)),
            pltpu.SemaphoreType.DMA((14,)),
        ],
        compiler_params=pltpu.CompilerParams(
            collective_id=0, has_side_effects=True, vmem_limit_bytes=48 * 1024 * 1024
        ),
        name="block",
    )(
        hidden_in,
        cotangent,
        coarse_state,
        edge_self,
        edge_peer,
        edge_out,
        coarse_self,
        coarse_peer,
        coarse_out,
        fine_nbrs.T,
        rim_rows.reshape(2, rim),
        send_lists,
        member_slots,
        own_slots.reshape(fine // 128, 128),
        coarse_nbrs.T,
    )
    plane, column = n_dom // 2, n_grp * 2
    rows = 6 * width // plane
    sums = pl.pallas_call(
        functools.partial(sum_kernel, n_grp, n_dom),
        out_shape=jax.ShapeDtypeStruct((6 * width, width), F32),
        in_specs=[vmem],
        out_specs=vmem,
        scratch_shapes=[
            pltpu.VMEM((plane, rows, width), F32),
            pltpu.VMEM((rows, width), F32),
            pltpu.VMEM((column, rows, width), F32),
            pltpu.SemaphoreType.DMA((2 * plane + column,)),
            pltpu.SemaphoreType.DMA((2 * plane + column,)),
        ],
        compiler_params=pltpu.CompilerParams(
            collective_id=1, has_side_effects=True, vmem_limit_bytes=16 * 1024 * 1024
        ),
        name="sums",
    )(grads)
    anywhere = pl.BlockSpec(memory_space=pl.ANY)
    square = jax.ShapeDtypeStruct((width, width), F32)
    return pl.pallas_call(
        finish_kernel,
        out_shape=(jax.ShapeDtypeStruct((fine, width), F32),) + (square,) * 6,
        in_specs=[anywhere] * 2,
        out_specs=(anywhere,) * 7,
        scratch_shapes=[pltpu.SemaphoreType.DMA((7,))],
        name="finish",
    )(node_grad, sums)


def solution(mesh):
    rows = P(("grp", "dom"), None)
    flat = P(("grp", "dom"))
    whole = P()
    in_specs = (rows,) * 3 + (whole,) * 6 + (rows, flat, rows, rows, flat, rows)
    out_specs = (rows,) + (whole,) * 6
    return jax.shard_map(
        functools.partial(body, mesh.shape["grp"], mesh.shape["dom"]),
        mesh=mesh,
        in_specs=in_specs,
        out_specs=out_specs,
        check_vma=False,
    )
```

```python
import functools

import jax
import jax.numpy as jnp
from jax import lax
from jax.experimental import pallas as pl
from jax.experimental.pallas import tpu as pltpu
from jax.sharding import PartitionSpec as P

MESH = pl.DeviceIdType.MESH
F32 = jnp.float32
BF16 = jnp.bfloat16
OFF = -1.0e4


def dot(a, b):
    return jnp.dot(a, b, preferred_element_type=F32)


def dot_nt(a, b):
    return lax.dot_general(a, b, (((1,), (1,)), ((), ())), preferred_element_type=F32)


def dot_tn(a, b):
    return lax.dot_general(a, b, (((0,), (0,)), ((), ())), preferred_element_type=F32)


def one_hot(index, shape, axis):
    ids = lax.broadcasted_iota(jnp.int32, shape, axis).astype(jnp.int16)
    hit = jnp.broadcast_to(index.astype(jnp.int16), shape) == ids
    return jnp.where(hit, jnp.ones(shape, BF16), jnp.zeros(shape, BF16))


def in_columns(index, width):
    return one_hot(index, (index.shape[0], width), 1)


def in_rows(index, height):
    return one_hot(index, (height, index.shape[1]), 0)


def split(values):
    high = values.astype(BF16)
    return high, (values - high.astype(F32)).astype(BF16)


def gate(pre):
    squash = 0.5 + 0.5 * jnp.tanh(0.5 * pre)
    act = pre * squash
    return act, squash + act * (1.0 - squash)


NAMES = 15


def block_kernel(n_grp, n_dom, *refs):
    inputs = refs[:NAMES]
    out_ref, grads_ref = refs[NAMES : NAMES + 2]
    held = refs[NAMES + 2 : 2 * NAMES + 2]
    (
        cot_out,
        cot_in,
        rep_out,
        rep_in,
        rim_out,
        rim_in,
        ret_out,
        ret_in,
        peer_hl,
        pre_self_ref,
        window,
        slope_ref,
        pooled_ref,
        place_ref,
        rim_sum,
        part_ref,
        first_a,
        first_b,
        mine_a,
        mine_b,
        second_a,
        second_b,
        load_sem,
        send_sem,
        recv_sem,
        sum_send,
        sum_recv,
    ) = refs[2 * NAMES + 2 :]
    (
        hidden_ref,
        cot_ref,
        coarse_ref,
        ws_ref,
        wp_ref,
        wo_ref,
        cws_ref,
        cwp_ref,
        cwo_ref,
        nbrs_ref,
        rim_ref,
        send_ref,
        member_ref,
        own_ref,
        cnbrs_ref,
    ) = held
    loads = [
        pltpu.make_async_copy(src, dst, load_sem.at[i])
        for i, (src, dst) in enumerate(zip(inputs, held))
    ]
    order = (11, 1, 10, 0, 12, 13, 2, 6, 7, 8, 14, 3, 4, 5, 9)
    for i in order:
        loads[i].start()

    grp = lax.axis_index("grp")
    me = lax.axis_index("dom")
    fine, width = hidden_ref.shape
    coarse = coarse_ref.shape[0]
    slots = nbrs_ref.shape[0]
    rim = rim_ref.shape[1]
    sends = send_ref.shape[1]
    block = min(512, fine)
    blocks = fine // block
    span = block + 2 * rim
    offsets = (1, -1, 2, -2, n_dom // 2)
    to = [lax.rem(me + (n_dom + o), n_dom) for o in offsets]
    source = [lax.rem(me + (n_dom - o), n_dom) for o in offsets]

    barrier = pltpu.get_barrier_semaphore()

    def greet_dom(t, carry):
        peer = (grp, lax.rem(me + t, n_dom))
        pl.semaphore_signal(barrier, inc=1, device_id=peer, device_id_type=MESH)
        return carry

    def greet_grp(t, carry):
        peer = (lax.rem(grp + t, n_grp), me)
        pl.semaphore_signal(barrier, inc=1, device_id=peer, device_id_type=MESH)
        return carry

    lax.fori_loop(1, n_dom, greet_dom, 0)
    lax.fori_loop(1, n_grp, greet_grp, 0)

    def remote(src, dst, index, peer):
        return pltpu.make_async_remote_copy(
            src_ref=src,
            dst_ref=dst,
            send_sem=send_sem.at[index],
            recv_sem=recv_sem.at[index],
            device_id=(grp, peer),
            device_id_type=MESH,
        )

    cot_copies = [remote(cot_out.at[k], cot_in.at[k], k, to[k]) for k in range(5)]
    rim_copies = [remote(rim_out.at[k], rim_in.at[k], 5 + k, to[k]) for k in range(2)]
    rep_copies = [remote(rep_out.at[k], rep_in.at[k], 7 + k, source[k]) for k in range(5)]
    ret_copies = [remote(ret_out.at[k], ret_in.at[k], 12 + k, to[k]) for k in range(2)]

    class Sum:
        def __init__(self, base, size, first, mine, second, sems):
            self.base, self.rows = base, size // n_dom
            self.first, self.mine, self.second, self.sems = first, mine, second, sems

        def copy(self, src, dst, index, peer):
            return pltpu.make_async_remote_copy(
                src_ref=src,
                dst_ref=dst,
                send_sem=sum_send.at[self.sems + index],
                recv_sem=sum_recv.at[self.sems + index],
                device_id=peer,
                device_id_type=MESH,
            )

        def cut(self, index):
            return pl.ds(pl.multiple_of(self.base + index * self.rows, 8), self.rows)

        def scatter(self, t):
            peer = lax.rem(me + t, n_dom)
            return self.copy(
                part_ref.at[self.cut(peer), :], self.first.at[me], t, (grp, peer)
            )

        def across(self, t):
            peer = lax.rem(grp + t, n_grp)
            return self.copy(self.mine, self.second.at[grp], n_dom + t, (peer, me))

        def gather(self, t):
            peer = lax.rem(me + t, n_dom)
            mine = grads_ref.at[self.cut(me), :]
            return self.copy(mine, mine, n_dom + n_grp + t, (grp, peer))

        def each(self, make, count, act):
            def step(t, carry):
                act(make(t))
                return carry

            lax.fori_loop(1, count, step, 0)

        def start_scatter(self):
            self.each(self.scatter, n_dom, lambda c: c.start())
            self.first[me] = part_ref[self.cut(me), :]

        def start_across(self):
            self.each(self.scatter, n_dom, lambda c: c.wait())
            total = self.first[0]
            for t in range(1, n_dom):
                total += self.first[t]
            self.mine[...] = total
            self.each(self.across, n_grp, lambda c: c.start())
            self.second[grp] = total

        def start_gather(self):
            self.each(self.across, n_grp, lambda c: c.wait())
            total = self.second[0]
            for t in range(1, n_grp):
                total += self.second[t]
            grads_ref[self.cut(me), :] = total
            self.each(self.gather, n_dom, lambda c: c.start())

        def finish(self):
            self.each(self.gather, n_dom, lambda c: c.wait())

    sum_a = Sum(2 * width, 4 * width, first_a, mine_a, second_a, 0)
    sum_b = Sum(0, 2 * width, first_b, mine_b, second_b, 2 * n_dom + n_grp)

    for i in (11, 10, 1):
        loads[i].wait()
    send_rows = [send_ref[pl.ds(t, 1), :] for t in to]
    listed = jnp.concatenate(
        send_rows + [rim_ref[1:2, :], rim_ref[0:1, :], jnp.zeros((1, sends), jnp.int32)], axis=0
    )
    listed_cols = listed.T
    for k in range(5):
        cot_out[k] = dot(in_columns(listed_cols[:, k : k + 1], fine), cot_ref[...]).astype(BF16)
    pl.semaphore_wait(barrier, n_dom + n_grp - 2)
    for copy in cot_copies:
        copy.start()
    loads[0].wait()
    for k in range(2):
        rim_out[k] = dot(in_columns(listed_cols[:, 5 + k : 6 + k], fine), hidden_ref[...]).astype(
            BF16
        )
    for copy in rim_copies:
        copy.start()
    for i in range(NAMES):
        if i not in (0, 1, 10, 11):
            loads[i].wait()
    member_rows = [member_ref[pl.ds(s, 1), :] for s in source]
    own_hot = jnp.concatenate(
        [in_rows(own_ref[t : t + 1, :], coarse) for t in range(fine // 128)], axis=1
    )
    far_hot = jnp.concatenate([in_rows(row, coarse) for row in member_rows], axis=1)
    own_pull = dot(own_hot, cot_ref[...])
    members = dot(own_hot, jnp.ones((fine, width), BF16)) + dot(
        far_hot, jnp.ones((5 * sends, width), BF16)
    )

    coarse_rows = coarse_ref[...]
    coarse_self = dot(coarse_rows, cws_ref[...])
    coarse_peer = jnp.concatenate(split(dot(coarse_rows, cwp_ref[...])), axis=1)
    links = cnbrs_ref[...]
    link_cols = links.T
    coarse_slopes = []
    coarse_pool = jnp.zeros((coarse, width), F32)
    for j in range(slots):
        col = link_cols[:, j : j + 1]
        got = dot(in_columns(col, coarse), coarse_peer)
        bias = jnp.where(col == coarse, OFF, 0.0)
        act, slope = gate(coarse_self + got[:, :width] + (got[:, width:] + bias))
        coarse_pool += act
        coarse_slopes.append(slope)
    coarse_pool = coarse_pool.astype(BF16)

    both = dot(hidden_ref[...], jnp.concatenate([ws_ref[...], wp_ref[...]], axis=1))
    pre_self_ref[...] = both[:, :width]
    high, low = split(both[:, width:])
    peer_hl[0:fine, 0:width] = high
    peer_hl[0:fine, width:] = low

    for copy in cot_copies:
        copy.wait()
    far_pull = dot(far_hot, cot_in[...].reshape(5 * sends, width))
    pulled = own_pull + far_pull
    pulled_b = pulled.astype(BF16)
    grad_pool = dot_nt(pulled_b, cwo_ref[...])
    grad_sum = jnp.zeros((coarse, width), F32)
    peer_sum = jnp.zeros((coarse, width), F32)
    for j in range(slots):
        grad_pre = grad_pool * coarse_slopes[j]
        grad_sum += grad_pre
        peer_sum += dot(in_rows(links[j : j + 1, :], coarse), grad_pre.astype(BF16))
    grad_sum = grad_sum.astype(BF16)
    high, low = split(peer_sum)
    node_grad = pulled + dot_nt(grad_sum, cws_ref[...])
    node_grad += dot_nt(high, cwp_ref[...]) + dot_nt(low, cwp_ref[...])
    back = (node_grad / members).astype(BF16)
    member_cols = jnp.concatenate(
        member_rows + [jnp.zeros((3, sends), jnp.int32)], axis=0
    ).T
    for k in range(5):
        rep_out[k] = dot(in_columns(member_cols[:, k : k + 1], coarse), back).astype(BF16)
    for copy in rep_copies:
        copy.start()
    part_ref[3 * width : 4 * width, :] = dot_tn(coarse_rows, grad_sum)
    part_ref[4 * width : 5 * width, :] = dot_tn(coarse_rows, high) + dot_tn(coarse_rows, low)
    part_ref[5 * width : 6 * width, :] = dot_tn(coarse_pool, pulled_b)

    for copy in rim_copies:
        copy.wait()
    lower = jnp.where(me > 0, 1.0, 0.0).astype(BF16)
    upper = jnp.where(me < n_dom - 1, 1.0, 0.0).astype(BF16)
    rims = jnp.concatenate([rim_in[0] * lower, rim_in[1] * upper], axis=0)
    high, low = split(dot(rims, wp_ref[...]))
    window[block:, 0:width] = high
    window[block:, width:] = low

    def forward(b, carry):
        first = pl.multiple_of(b * block, block)
        here = pl.ds(first, block)
        picked = nbrs_ref[:, here]
        placed = jnp.where(picked < fine, picked - first, picked - fine + block)
        place_ref[b] = placed
        cols = placed.T
        window[0:block, :] = peer_hl[here, :]
        own_pre = pre_self_ref[here, :]
        total = jnp.zeros((block, width), F32)
        for j in range(slots):
            col = cols[:, j : j + 1]
            got = dot(in_columns(col, span), window[...])
            bias = jnp.where(col == span, OFF, 0.0)
            act, slope = gate(own_pre + got[:, :width] + (got[:, width:] + bias))
            total += act
            slope_ref[b, j] = slope
        pooled_ref[here, :] = total.astype(BF16)
        return carry

    lax.fori_loop(0, blocks, forward, 0)

    for copy in rep_copies:
        copy.wait()
    sources = jnp.concatenate([back, rep_in[...].reshape(5 * sends, width)], axis=0)
    part_ref[0 : 3 * width, :] = jnp.zeros((3 * width, width), F32)
    rim_sum[...] = jnp.zeros((2 * rim, width), F32)
    self_weight = ws_ref[...]
    peer_weight = wp_ref[...]
    out_weight = wo_ref[...]

    def arrive(b, carry):
        first = pl.multiple_of(b * block, block)
        here = pl.ds(first, block)
        own_hots = jnp.concatenate(
            [
                in_columns(own_ref[pl.ds(b * (block // 128) + t, 1), :].T, coarse)
                for t in range(block // 128)
            ],
            axis=0,
        )
        hots = jnp.concatenate([own_hots] + [in_rows(row - first, block) for row in send_rows], axis=1)
        arriving = cot_ref[here, :].astype(F32) + dot(hots, sources)
        out_ref[here, :] = arriving
        part_ref[2 * width : 3 * width, :] += dot_tn(pooled_ref[here, :], arriving.astype(BF16))
        return carry

    lax.fori_loop(0, blocks, arrive, 0)
    sum_a.start_scatter()

    def backward(b, carry):
        first = pl.multiple_of(b * block, block)
        here = pl.ds(first, block)
        arriving = out_ref[here, :]
        grad_pool = dot_nt(arriving.astype(BF16), out_weight)
        grad_sum = jnp.zeros((block, width), F32)
        peer_sum = jnp.zeros((span, width), F32)
        placed = place_ref[b]
        for j in range(slots):
            grad_pre = grad_pool * slope_ref[b, j]
            grad_sum += grad_pre
            peer_sum += dot(in_rows(placed[j : j + 1, :], span), grad_pre.astype(BF16))
        grad_sum = grad_sum.astype(BF16)
        rim_sum[...] += peer_sum[block:]
        high, low = split(peer_sum[:block])
        rows = hidden_ref[here, :]
        got = dot_tn(rows, jnp.concatenate([grad_sum, high, low], axis=1))
        part_ref[0:width, :] += got[:, :width]
        part_ref[width : 2 * width, :] += got[:, width : 2 * width] + got[:, 2 * width :]
        out_ref[here, :] = (
            arriving
            + dot_nt(grad_sum, self_weight)
            + dot_nt(high, peer_weight)
            + dot_nt(low, peer_weight)
        )
        return carry

    half = max(blocks // 2, 1)
    lax.fori_loop(0, half, backward, 0)
    sum_a.start_across()
    lax.fori_loop(half, blocks, backward, 0)
    sum_a.start_gather()

    high, low = split(rim_sum[...])
    part_ref[width : 2 * width, :] += dot_tn(rims, high) + dot_tn(rims, low)
    sum_b.start_scatter()
    rim_grad = (dot_nt(high, peer_weight) + dot_nt(low, peer_weight)).astype(BF16)
    ret_out[0] = rim_grad[rim:]
    ret_out[1] = rim_grad[:rim]
    for copy in ret_copies:
        copy.start()
    sum_b.start_across()
    for copy in ret_copies:
        copy.wait()
    returned = jnp.concatenate([ret_in[0] * lower, ret_in[1] * upper], axis=0)

    def give_back(b, carry):
        first = pl.multiple_of(b * block, block)
        here = pl.ds(first, block)
        hots = jnp.concatenate([in_rows(rim_ref[k : k + 1, :] - first, block) for k in range(2)], axis=1)
        out_ref[here, :] += dot(hots, returned)
        return carry

    lax.fori_loop(0, blocks, give_back, 0)
    sum_b.start_gather()
    sum_a.finish()
    sum_b.finish()


def finish_kernel(node_ref, sums_ref, out_ref, *rest):
    parts, sem = rest[:-1], rest[-1]
    width = sums_ref.shape[1]
    copies = [pltpu.make_async_copy(node_ref, out_ref, sem.at[6])]
    for k, part in enumerate(parts):
        copies.append(
            pltpu.make_async_copy(sums_ref.at[pl.ds(k * width, width), :], part, sem.at[k])
        )
    for copy in copies:
        copy.start()
    for copy in copies:
        copy.wait()


def body(
    n_grp,
    n_dom,
    hidden_in,
    cotangent,
    coarse_state,
    edge_self,
    edge_peer,
    edge_out,
    coarse_self,
    coarse_peer,
    coarse_out,
    fine_nbrs,
    rim_rows,
    send_lists,
    member_slots,
    own_slots,
    coarse_nbrs,
):
    fine, width = hidden_in.shape
    coarse = coarse_state.shape[0]
    slots = fine_nbrs.shape[1]
    rim = rim_rows.shape[0] // 2
    sends = send_lists.shape[1]
    block = min(512, fine)
    blocks = fine // block
    vmem = pl.BlockSpec(memory_space=pltpu.VMEM)
    anywhere = pl.BlockSpec(memory_space=pl.ANY)
    args = (
        hidden_in,
        cotangent,
        coarse_state,
        edge_self,
        edge_peer,
        edge_out,
        coarse_self,
        coarse_peer,
        coarse_out,
        fine_nbrs.T,
        rim_rows.reshape(2, rim),
        send_lists,
        member_slots,
        own_slots.reshape(fine // 128, 128),
        coarse_nbrs.T,
    )
    sum_sems = 2 * (2 * n_dom + n_grp)
    node_grad, sums = pl.pallas_call(
        functools.partial(block_kernel, n_grp, n_dom),
        out_shape=(
            jax.ShapeDtypeStruct((fine, width), F32),
            jax.ShapeDtypeStruct((6 * width, width), F32),
        ),
        in_specs=[anywhere] * NAMES,
        out_specs=(vmem, vmem),
        scratch_shapes=[pltpu.VMEM(a.shape, a.dtype) for a in args]
        + [pltpu.VMEM((5, sends, width), BF16)] * 4
        + [pltpu.VMEM((2, rim, width), BF16)] * 4
        + [
            pltpu.VMEM((fine, 2 * width), BF16),
            pltpu.VMEM((fine, width), F32),
            pltpu.VMEM((block + 2 * rim, 2 * width), BF16),
            pltpu.VMEM((blocks, slots, block, width), F32),
            pltpu.VMEM((fine, width), BF16),
            pltpu.VMEM((blocks, slots, block), jnp.int32),
            pltpu.VMEM((2 * rim, width), F32),
            pltpu.VMEM((6 * width, width), F32),
            pltpu.VMEM((n_dom, 4 * width // n_dom, width), F32),
            pltpu.VMEM((n_dom, 2 * width // n_dom, width), F32),
            pltpu.VMEM((4 * width // n_dom, width), F32),
            pltpu.VMEM((2 * width // n_dom, width), F32),
            pltpu.VMEM((n_grp, 4 * width // n_dom, width), F32),
            pltpu.VMEM((n_grp, 2 * width // n_dom, width), F32),
            pltpu.SemaphoreType.DMA((NAMES,)),
            pltpu.SemaphoreType.DMA((14,)),
            pltpu.SemaphoreType.DMA((14,)),
            pltpu.SemaphoreType.DMA((sum_sems,)),
            pltpu.SemaphoreType.DMA((sum_sems,)),
        ],
        compiler_params=pltpu.CompilerParams(
            collective_id=0, has_side_effects=True, vmem_limit_bytes=56 * 1024 * 1024
        ),
        name="block",
    )(*args)
    square = jax.ShapeDtypeStruct((width, width), F32)
    return pl.pallas_call(
        finish_kernel,
        out_shape=(jax.ShapeDtypeStruct((fine, width), F32),) + (square,) * 6,
        in_specs=[vmem] * 2,
        out_specs=(anywhere,) * 7,
        scratch_shapes=[pltpu.SemaphoreType.DMA((7,))],
        name="finish",
    )(node_grad, sums)


def solution(mesh):
    rows = P(("grp", "dom"), None)
    flat = P(("grp", "dom"))
    whole = P()
    in_specs = (rows,) * 3 + (whole,) * 6 + (rows, flat, rows, rows, flat, rows)
    out_specs = (rows,) + (whole,) * 6
    return jax.shard_map(
        functools.partial(body, mesh.shape["grp"], mesh.shape["dom"]),
        mesh=mesh,
        in_specs=in_specs,
        out_specs=out_specs,
        check_vma=False,
    )
```

```python
import functools

import jax
import jax.numpy as jnp
from jax import lax
from jax.experimental import pallas as pl
from jax.experimental.pallas import tpu as pltpu
from jax.sharding import PartitionSpec as P

MESH = pl.DeviceIdType.MESH
F32 = jnp.float32
BF16 = jnp.bfloat16
OFF = -1.0e4
TILE = 256


def dot(a, b):
    return jnp.dot(a, b, preferred_element_type=F32)


def dot_nt(a, b):
    return lax.dot_general(a, b, (((1,), (1,)), ((), ())), preferred_element_type=F32)


def dot_tn(a, b):
    return lax.dot_general(a, b, (((0,), (0,)), ((), ())), preferred_element_type=F32)


def one_hot(index, shape, axis):
    ids = lax.broadcasted_iota(jnp.int32, shape, axis).astype(jnp.int16)
    hit = jnp.broadcast_to(index.astype(jnp.int16), shape) == ids
    return jnp.where(hit, jnp.ones(shape, BF16), jnp.zeros(shape, BF16))


def in_columns(index, width):
    return one_hot(index, (index.shape[0], width), 1)


def in_rows(index, height):
    return one_hot(index, (height, index.shape[1]), 0)


def split(values):
    high = values.astype(BF16)
    return high, (values - high.astype(F32)).astype(BF16)


def gate(half):
    tilt = jnp.tanh(half)
    both = 1.0 + tilt
    act = half * both
    return act, both + act * (2.0 - both)


NAMES = 15


def block_kernel(n_grp, n_dom, *refs):
    inputs = refs[:NAMES]
    out_ref, grads_ref = refs[NAMES : NAMES + 2]
    held = refs[NAMES + 2 : 2 * NAMES + 2]
    (
        cot_out,
        cot_in,
        rep_out,
        rep_in,
        rim_out,
        rim_in,
        ret_out,
        ret_in,
        hots,
        table_ref,
        own_half,
        slope_ref,
        pooled_ref,
        up_ref,
        grad_ref,
        rim_sum,
        part_ref,
        first_a,
        first_b,
        mine_a,
        mine_b,
        second_a,
        second_b,
        load_sem,
        send_sem,
        recv_sem,
        sum_send,
        sum_recv,
    ) = refs[2 * NAMES + 2 :]
    (
        hidden_ref,
        cot_ref,
        coarse_ref,
        ws_ref,
        wp_ref,
        wo_ref,
        cws_ref,
        cwp_ref,
        cwo_ref,
        nbrs_ref,
        rim_ref,
        send_ref,
        member_ref,
        own_ref,
        cnbrs_ref,
    ) = held
    loads = [
        pltpu.make_async_copy(src, dst, load_sem.at[i])
        for i, (src, dst) in enumerate(zip(inputs, held))
    ]
    grp = lax.axis_index("grp")
    me = lax.axis_index("dom")
    fine, width = hidden_ref.shape
    coarse = coarse_ref.shape[0]
    slots = nbrs_ref.shape[0]
    rim = rim_ref.shape[1]
    sends = send_ref.shape[1]
    block = min(512, fine)
    blocks = fine // block
    halves = block // TILE
    groups = halves + 2 * rim // TILE
    offsets = (1, -1, 2, -2, n_dom // 2)
    to = [lax.rem(me + (n_dom + o), n_dom) for o in offsets]
    source = [lax.rem(me + (n_dom - o), n_dom) for o in offsets]

    barrier = pltpu.get_barrier_semaphore()

    for peer in to:
        pl.semaphore_signal(barrier, inc=1, device_id=(grp, peer), device_id_type=MESH)
    order = (11, 1, 10, 0, 12, 13, 2, 6, 7, 8, 14, 3, 4, 5, 9)
    for i in order:
        loads[i].start()

    def greet_dom(t, carry):
        peer = (grp, lax.rem(me + t, n_dom))
        pl.semaphore_signal(barrier, inc=1, device_id=peer, device_id_type=MESH)
        return carry

    def greet_grp(t, carry):
        peer = (lax.rem(grp + t, n_grp), me)
        pl.semaphore_signal(barrier, inc=1, device_id=peer, device_id_type=MESH)
        return carry

    lax.fori_loop(3, n_dom // 2, greet_dom, 0)
    lax.fori_loop(n_dom // 2 + 1, n_dom - 2, greet_dom, 0)
    lax.fori_loop(1, n_grp, greet_grp, 0)

    def remote(src, dst, index, peer):
        return pltpu.make_async_remote_copy(
            src_ref=src,
            dst_ref=dst,
            send_sem=send_sem.at[index],
            recv_sem=recv_sem.at[index],
            device_id=(grp, peer),
            device_id_type=MESH,
        )

    cot_copies = [remote(cot_out.at[k], cot_in.at[k], k, to[k]) for k in range(5)]
    rim_copies = [remote(rim_out.at[k], rim_in.at[k], 5 + k, to[k]) for k in range(2)]
    rep_copies = [remote(rep_out.at[k], rep_in.at[k], 7 + k, source[k]) for k in range(5)]
    ret_copies = [remote(ret_out.at[k], ret_in.at[k], 12 + k, to[k]) for k in range(2)]

    class Sum:
        def __init__(self, base, size, first, mine, second, sems):
            self.base, self.rows = base, size // n_dom
            self.first, self.mine, self.second, self.sems = first, mine, second, sems

        def copy(self, src, dst, index, peer):
            return pltpu.make_async_remote_copy(
                src_ref=src,
                dst_ref=dst,
                send_sem=sum_send.at[self.sems + index],
                recv_sem=sum_recv.at[self.sems + index],
                device_id=peer,
                device_id_type=MESH,
            )

        def cut(self, index):
            return pl.ds(pl.multiple_of(self.base + index * self.rows, 8), self.rows)

        def scatter(self, t):
            peer = lax.rem(me + t, n_dom)
            return self.copy(
                part_ref.at[self.cut(peer), :], self.first.at[me], t, (grp, peer)
            )

        def across(self, t):
            peer = lax.rem(grp + t, n_grp)
            return self.copy(self.mine, self.second.at[grp], n_dom + t, (peer, me))

        def gather(self, t):
            peer = lax.rem(me + t, n_dom)
            mine = grads_ref.at[self.cut(me), :]
            return self.copy(mine, mine, n_dom + n_grp + t, (grp, peer))

        def each(self, make, count, act):
            def step(t, carry):
                act(make(t))
                return carry

            lax.fori_loop(1, count, step, 0)

        def start_scatter(self):
            self.each(self.scatter, n_dom, lambda c: c.start())
            self.first[me] = part_ref[self.cut(me), :]

        def start_across(self):
            self.each(self.scatter, n_dom, lambda c: c.wait_recv())
            total = self.first[0]
            for t in range(1, n_dom):
                total += self.first[t]
            self.mine[...] = total
            self.each(self.across, n_grp, lambda c: c.start())
            self.second[grp] = total

        def start_gather(self):
            self.each(self.across, n_grp, lambda c: c.wait_recv())
            total = self.second[0]
            for t in range(1, n_grp):
                total += self.second[t]
            grads_ref[self.cut(me), :] = total
            self.each(self.gather, n_dom, lambda c: c.start())

        def finish(self):
            self.each(self.gather, n_dom, lambda c: c.wait_recv())
            self.each(self.scatter, n_dom, lambda c: c.wait_send())
            self.each(self.across, n_grp, lambda c: c.wait_send())
            self.each(self.gather, n_dom, lambda c: c.wait_send())

    sum_a = Sum(2 * width, 4 * width, first_a, mine_a, second_a, 0)
    sum_b = Sum(0, 2 * width, first_b, mine_b, second_b, 2 * n_dom + n_grp)

    for i in (11, 10, 1):
        loads[i].wait()
    send_rows = [send_ref[pl.ds(t, 1), :] for t in to]
    listed = jnp.concatenate(
        send_rows + [rim_ref[1:2, :], rim_ref[0:1, :], jnp.zeros((1, sends), jnp.int32)], axis=0
    )
    listed_cols = listed.T
    sent = coarse + 5 * sends
    for step, k in enumerate((4, 2, 3, 0, 1)):
        hot = in_columns(listed_cols[:, k : k + 1], fine)
        hots[coarse + k * sends : coarse + (k + 1) * sends, :] = hot
        cot_out[k] = dot(hot, cot_ref[...]).astype(BF16)
        if step == 0:
            pl.semaphore_wait(barrier, n_dom + n_grp - 2)
        cot_copies[k].start()
    loads[0].wait()
    for k in range(2):
        hots[sent + k * rim : sent + (k + 1) * rim, :] = in_columns(
            listed_cols[:, 5 + k : 6 + k], fine
        )
    chosen = dot(hots[sent:, :], hidden_ref[...]).astype(BF16)
    for k in range(2):
        rim_out[k] = chosen[k * rim : (k + 1) * rim]
    for copy in rim_copies:
        copy.start()
    for i in range(NAMES):
        if i not in (0, 1, 10, 11):
            loads[i].wait()
    member_rows = [member_ref[pl.ds(s, 1), :] for s in source]

    for t in range(fine // 128):
        hots[0:coarse, t * 128 : (t + 1) * 128] = in_rows(own_ref[t : t + 1, :], coarse)
    far_hot = jnp.concatenate([in_rows(row, coarse) for row in member_rows], axis=1)
    own_pull = dot(
        hots[0:coarse, :], jnp.concatenate([cot_ref[...], jnp.ones((fine, width), BF16)], axis=1)
    )

    coarse_rows = coarse_ref[...]
    coarse_self = 0.5 * dot(coarse_rows, cws_ref[...])
    coarse_peer = jnp.concatenate(split(0.5 * dot(coarse_rows, cwp_ref[...])), axis=1)
    links = cnbrs_ref[...]
    link_cols = links.T
    coarse_slopes = []
    coarse_pool = jnp.zeros((coarse, width), F32)
    for j in range(slots):
        col = link_cols[:, j : j + 1]
        got = dot(in_columns(col, coarse), coarse_peer)
        bias = jnp.where(col == coarse, OFF, 0.0)
        act, slope = gate(coarse_self + got[:, :width] + (got[:, width:] + bias))
        coarse_pool += act
        coarse_slopes.append(slope)
    coarse_pool = coarse_pool.astype(BF16)
    link_hot = jnp.concatenate([in_rows(links[j : j + 1, :], coarse) for j in range(slots)], axis=1)

    for copy in cot_copies:
        copy.wait()
    arrived = cot_in[...].reshape(5 * sends, width)
    far_pull = dot(
        far_hot, jnp.concatenate([arrived, jnp.ones((5 * sends, width), BF16)], axis=1)
    )
    gathered = own_pull + far_pull
    pulled = gathered[:, :width]
    members = gathered[:, width:]
    pulled_b = pulled.astype(BF16)
    grad_pool = 0.5 * dot_nt(pulled_b, cwo_ref[...])
    grad_sum = jnp.zeros((coarse, width), F32)
    grad_pres = []
    for j in range(slots):
        grad_pre = grad_pool * coarse_slopes[j]
        grad_sum += grad_pre
        grad_pres.append(grad_pre.astype(BF16))
    grad_sum = grad_sum.astype(BF16)
    high, low = split(dot(link_hot, jnp.concatenate(grad_pres, axis=0)))
    node_grad = pulled + dot_nt(
        jnp.concatenate([grad_sum, high, low], axis=1),
        jnp.concatenate([cws_ref[...], cwp_ref[...], cwp_ref[...]], axis=1),
    )
    back = (node_grad / members).T.astype(BF16)
    replies = dot(back, far_hot).astype(BF16)
    for k in range(5):
        rep_out[k] = replies[:, k * sends : (k + 1) * sends]
    for copy in rep_copies:
        copy.start()
    part_ref[3 * width : 4 * width, :] = dot_tn(coarse_rows, grad_sum)
    part_ref[4 * width : 5 * width, :] = dot_tn(coarse_rows, high) + dot_tn(coarse_rows, low)
    part_ref[5 * width : 6 * width, :] = dot_tn(coarse_pool, pulled_b)

    self_turned = ws_ref[...].T
    peer_turned = wp_ref[...].T
    both_turned = jnp.concatenate([self_turned, peer_turned], axis=0)
    for t in range(fine // TILE):
        here = slice(t * TILE, (t + 1) * TILE)
        both = 0.5 * dot_nt(both_turned, hidden_ref[here, :])
        own_half[:, here] = both[:width]
        table_ref[t] = both[width:].astype(BF16)
        up_ref[:, here] = cot_ref[here, :].astype(F32).T

    for copy in rim_copies:
        copy.wait()
    lower = jnp.where(me > 0, 1.0, 0.0).astype(BF16)
    upper = jnp.where(me < n_dom - 1, 1.0, 0.0).astype(BF16)
    rims = jnp.concatenate([rim_in[0] * lower, rim_in[1] * upper], axis=0)
    for t in range(2 * rim // TILE):
        here = slice(t * TILE, (t + 1) * TILE)
        table_ref[fine // TILE + t] = (0.5 * dot_nt(peer_turned, rims[here])).astype(BF16)

    def places(b):
        first = pl.multiple_of(b * block, block)
        picked = nbrs_ref[:, pl.ds(first, block)]
        placed = jnp.where(picked < fine, picked - first, picked - (fine - block))
        return placed % TILE, placed // TILE

    def forward(b, carry):
        here = pl.ds(pl.multiple_of(b * block, block), block)
        near, far = places(b)
        table = jnp.concatenate(
            [table_ref[b * halves + t] for t in range(halves)]
            + [table_ref[fine // TILE + t] for t in range(2 * rim // TILE)],
            axis=0,
        )
        own = own_half[:, here]
        total = jnp.zeros((width, block), F32)
        for j in range(slots):
            got = dot(table, in_rows(near[j : j + 1, :], TILE))
            group = jnp.broadcast_to(far[j : j + 1, :], (width, block))
            peer = jnp.full((width, block), OFF, F32)
            for t in range(groups):
                peer = jnp.where(group == t, got[t * width : (t + 1) * width], peer)
            act, slope = gate(own + peer)
            total += act
            slope_ref[b, j] = slope
        pooled_ref[:, here] = total.astype(BF16)
        return carry

    lax.fori_loop(0, blocks, forward, 0)

    for copy in rep_copies:
        copy.wait()
    sources = jnp.concatenate([back] + [rep_in[k] for k in range(5)], axis=1)

    def arrive(b, carry):
        here = pl.ds(pl.multiple_of(b * block, block), block)
        up_ref[:, here] += dot(sources, hots[0:sent, here])
        return carry

    lax.fori_loop(0, blocks, arrive, 0)
    part_ref[2 * width : 3 * width, :] = dot_nt(pooled_ref[...], up_ref[...].astype(BF16))
    sum_a.start_scatter()
    rim_sum[...] = jnp.zeros((width, 2 * rim), F32)
    self_weight = ws_ref[...]
    peer_weight = wp_ref[...]
    out_weight = wo_ref[...]

    def backward(b, carry):
        first = pl.multiple_of(b * block, block)
        here = pl.ds(first, block)
        near, far = places(b)
        near_cols = near.T
        grad_pool = 0.5 * dot(out_weight, up_ref[:, here].astype(BF16))
        grad_sum = jnp.zeros((width, block), F32)
        peer_sum = jnp.zeros((groups * width, TILE), F32)
        for j in range(slots):
            grad_pre = grad_pool * slope_ref[b, j]
            grad_sum += grad_pre
            grad_b = grad_pre.astype(BF16)
            group = jnp.broadcast_to(far[j : j + 1, :].astype(jnp.int16), (width, block))
            zero = jnp.zeros((width, block), BF16)
            spread = jnp.concatenate(
                [jnp.where(group == t, grad_b, zero) for t in range(groups)], axis=0
            )
            peer_sum += dot(spread, in_columns(near_cols[:, j : j + 1], TILE))
        grad_ref[0:width, here] = grad_sum.astype(BF16)
        for t in range(halves):
            high, low = split(peer_sum[t * width : (t + 1) * width])
            cut = pl.ds(pl.multiple_of(first + t * TILE, TILE), TILE)
            grad_ref[width : 2 * width, cut] = high
            grad_ref[2 * width : 3 * width, cut] = low
        rim_sum[...] += jnp.concatenate(
            [peer_sum[t * width : (t + 1) * width] for t in range(halves, groups)], axis=1
        )
        return carry

    lax.fori_loop(0, blocks, backward, 0)

    high, low = split(rim_sum[...])
    turned = dot(grad_ref[...], hidden_ref[...])
    peer_grad = turned[width : 2 * width] + turned[2 * width :] + dot(high, rims) + dot(low, rims)
    part_ref[0:width, :] = turned[:width].T
    part_ref[width : 2 * width, :] = peer_grad.T
    sum_b.start_scatter()
    sum_a.start_across()
    rim_grad = (dot(peer_weight, high) + dot(peer_weight, low)).astype(BF16)
    ret_out[0] = rim_grad[:, rim:]
    ret_out[1] = rim_grad[:, :rim]
    for copy in ret_copies:
        copy.start()
    weights = jnp.concatenate([self_weight, peer_weight, peer_weight], axis=1)

    def own_part(b, carry):
        here = pl.ds(pl.multiple_of(b * block, block), block)
        up_ref[:, here] += dot(weights, grad_ref[:, here])
        return carry

    lax.fori_loop(0, blocks, own_part, 0)
    sum_b.start_across()
    sum_a.start_gather()
    for copy in ret_copies:
        copy.wait()
    returned = jnp.concatenate([ret_in[1] * upper, ret_in[0] * lower], axis=1)

    def give_back(b, carry):
        here = pl.ds(pl.multiple_of(b * block, block), block)
        out_ref[here, :] = (up_ref[:, here] + dot(returned, hots[sent:, here])).T
        return carry

    lax.fori_loop(0, blocks, give_back, 0)
    sum_b.start_gather()
    sum_a.finish()
    sum_b.finish()


def finish_kernel(node_ref, sums_ref, out_ref, *rest):
    parts, sem = rest[:-1], rest[-1]
    width = sums_ref.shape[1]
    copies = [pltpu.make_async_copy(node_ref, out_ref, sem.at[6])]
    for k, part in enumerate(parts):
        copies.append(
            pltpu.make_async_copy(sums_ref.at[pl.ds(k * width, width), :], part, sem.at[k])
        )
    for copy in copies:
        copy.start()
    for copy in copies:
        copy.wait()


def body(
    n_grp,
    n_dom,
    hidden_in,
    cotangent,
    coarse_state,
    edge_self,
    edge_peer,
    edge_out,
    coarse_self,
    coarse_peer,
    coarse_out,
    fine_nbrs,
    rim_rows,
    send_lists,
    member_slots,
    own_slots,
    coarse_nbrs,
):
    fine, width = hidden_in.shape
    coarse = coarse_state.shape[0]
    slots = fine_nbrs.shape[1]
    rim = rim_rows.shape[0] // 2
    sends = send_lists.shape[1]
    block = min(512, fine)
    blocks = fine // block
    vmem = pl.BlockSpec(memory_space=pltpu.VMEM)
    anywhere = pl.BlockSpec(memory_space=pl.ANY)
    args = (
        hidden_in,
        cotangent,
        coarse_state,
        edge_self,
        edge_peer,
        edge_out,
        coarse_self,
        coarse_peer,
        coarse_out,
        fine_nbrs.T,
        rim_rows.reshape(2, rim),
        send_lists,
        member_slots,
        own_slots.reshape(fine // 128, 128),
        coarse_nbrs.T,
    )
    sum_sems = 2 * (2 * n_dom + n_grp)
    node_grad, sums = pl.pallas_call(
        functools.partial(block_kernel, n_grp, n_dom),
        out_shape=(
            jax.ShapeDtypeStruct((fine, width), F32),
            jax.ShapeDtypeStruct((6 * width, width), F32),
        ),
        in_specs=[anywhere] * NAMES,
        out_specs=(vmem, vmem),
        scratch_shapes=[pltpu.VMEM(a.shape, a.dtype) for a in args]
        + [pltpu.VMEM((5, sends, width), BF16)] * 4
        + [pltpu.VMEM((2, rim, width), BF16)] * 4
        + [
            pltpu.VMEM((coarse + 5 * sends + 2 * rim, fine), BF16),
            pltpu.VMEM(((fine + 2 * rim) // TILE, width, TILE), BF16),
            pltpu.VMEM((width, fine), F32),
            pltpu.VMEM((blocks, slots, width, block), F32),
            pltpu.VMEM((width, fine), BF16),
            pltpu.VMEM((width, fine), F32),
            pltpu.VMEM((3 * width, fine), BF16),
            pltpu.VMEM((width, 2 * rim), F32),
            pltpu.VMEM((6 * width, width), F32),
            pltpu.VMEM((n_dom, 4 * width // n_dom, width), F32),
            pltpu.VMEM((n_dom, 2 * width // n_dom, width), F32),
            pltpu.VMEM((4 * width // n_dom, width), F32),
            pltpu.VMEM((2 * width // n_dom, width), F32),
            pltpu.VMEM((n_grp, 4 * width // n_dom, width), F32),
            pltpu.VMEM((n_grp, 2 * width // n_dom, width), F32),
            pltpu.SemaphoreType.DMA((NAMES,)),
            pltpu.SemaphoreType.DMA((14,)),
            pltpu.SemaphoreType.DMA((14,)),
            pltpu.SemaphoreType.DMA((sum_sems,)),
            pltpu.SemaphoreType.DMA((sum_sems,)),
        ],
        compiler_params=pltpu.CompilerParams(
            collective_id=0, has_side_effects=True, vmem_limit_bytes=56 * 1024 * 1024
        ),
        name="block",
    )(*args)
    square = jax.ShapeDtypeStruct((width, width), F32)
    return pl.pallas_call(
        finish_kernel,
        out_shape=(jax.ShapeDtypeStruct((fine, width), F32),) + (square,) * 6,
        in_specs=[vmem] * 2,
        out_specs=(anywhere,) * 7,
        scratch_shapes=[pltpu.SemaphoreType.DMA((7,))],
        name="finish",
    )(node_grad, sums)


def solution(mesh):
    rows = P(("grp", "dom"), None)
    flat = P(("grp", "dom"))
    whole = P()
    in_specs = (rows,) * 3 + (whole,) * 6 + (rows, flat, rows, rows, flat, rows)
    out_specs = (rows,) + (whole,) * 6
    return jax.shard_map(
        functools.partial(body, mesh.shape["grp"], mesh.shape["dom"]),
        mesh=mesh,
        in_specs=in_specs,
        out_specs=out_specs,
        check_vma=False,
    )
```

```python
import functools

import jax
import jax.numpy as jnp
from jax import lax
from jax.experimental import pallas as pl
from jax.experimental.pallas import tpu as pltpu
from jax.sharding import PartitionSpec as P

MESH = pl.DeviceIdType.MESH
F32 = jnp.float32
BF16 = jnp.bfloat16
OFF = -1.0e4
TILE = 256


def dot(a, b):
    return jnp.dot(a, b, preferred_element_type=F32)


def dot_nt(a, b):
    return lax.dot_general(a, b, (((1,), (1,)), ((), ())), preferred_element_type=F32)


def dot_tn(a, b):
    return lax.dot_general(a, b, (((0,), (0,)), ((), ())), preferred_element_type=F32)


def one_hot(index, shape, axis):
    ids = lax.broadcasted_iota(jnp.int32, shape, axis).astype(jnp.int16)
    hit = jnp.broadcast_to(index.astype(jnp.int16), shape) == ids
    return jnp.where(hit, jnp.ones(shape, BF16), jnp.zeros(shape, BF16))


def in_columns(index, width):
    return one_hot(index, (index.shape[0], width), 1)


def in_rows(index, height):
    return one_hot(index, (height, index.shape[1]), 0)


def split(values):
    high = values.astype(BF16)
    return high, (values - high.astype(F32)).astype(BF16)


def gate(half):
    tilt = jnp.tanh(half)
    both = 1.0 + tilt
    act = half * both
    return act, both + act * (2.0 - both)


NAMES = 15


def block_kernel(n_grp, n_dom, *refs):
    inputs = refs[:NAMES]
    out_ref, grads_ref = refs[NAMES : NAMES + 2]
    held = refs[NAMES + 2 : 2 * NAMES + 2]
    (
        cot_out,
        cot_in,
        rep_out,
        rep_in,
        rim_out,
        rim_in,
        ret_out,
        ret_in,
        hots,
        table_ref,
        own_half,
        slope_ref,
        pooled_ref,
        up_ref,
        grad_ref,
        rim_sum,
        part_ref,
        first_a,
        first_b,
        mine_a,
        mine_b,
        second_a,
        second_b,
        load_sem,
        send_sem,
        recv_sem,
        sum_send,
        sum_recv,
    ) = refs[2 * NAMES + 2 :]
    (
        hidden_ref,
        cot_ref,
        coarse_ref,
        ws_ref,
        wp_ref,
        wo_ref,
        cws_ref,
        cwp_ref,
        cwo_ref,
        nbrs_ref,
        rim_ref,
        send_ref,
        member_ref,
        own_ref,
        cnbrs_ref,
    ) = held
    loads = [
        pltpu.make_async_copy(src, dst, load_sem.at[i])
        for i, (src, dst) in enumerate(zip(inputs, held))
    ]
    grp = lax.axis_index("grp")
    me = lax.axis_index("dom")
    fine, width = hidden_ref.shape
    coarse = coarse_ref.shape[0]
    slots = nbrs_ref.shape[0]
    rim = rim_ref.shape[1]
    sends = send_ref.shape[1]
    block = min(512, fine)
    blocks = fine // block
    halves = block // TILE
    groups = halves + 2 * rim // TILE
    offsets = (1, -1, 2, -2, n_dom // 2)
    to = [lax.rem(me + (n_dom + o), n_dom) for o in offsets]
    source = [lax.rem(me + (n_dom - o), n_dom) for o in offsets]

    barrier = pltpu.get_barrier_semaphore()

    for peer in to:
        pl.semaphore_signal(barrier, inc=1, device_id=(grp, peer), device_id_type=MESH)
    order = (11, 1, 10, 0, 12, 13, 2, 6, 7, 8, 14, 3, 4, 5, 9)
    for i in order:
        loads[i].start()

    def greet_dom(t, carry):
        peer = (grp, lax.rem(me + t, n_dom))
        pl.semaphore_signal(barrier, inc=1, device_id=peer, device_id_type=MESH)
        return carry

    def greet_grp(t, carry):
        peer = (lax.rem(grp + t, n_grp), me)
        pl.semaphore_signal(barrier, inc=1, device_id=peer, device_id_type=MESH)
        return carry

    lax.fori_loop(3, n_dom // 2, greet_dom, 0)
    lax.fori_loop(n_dom // 2 + 1, n_dom - 2, greet_dom, 0)
    lax.fori_loop(1, n_grp, greet_grp, 0)

    def remote(src, dst, index, peer):
        return pltpu.make_async_remote_copy(
            src_ref=src,
            dst_ref=dst,
            send_sem=send_sem.at[index],
            recv_sem=recv_sem.at[index],
            device_id=(grp, peer),
            device_id_type=MESH,
        )

    cot_copies = [remote(cot_out.at[k], cot_in.at[k], k, to[k]) for k in range(5)]
    rim_copies = [remote(rim_out.at[k], rim_in.at[k], 5 + k, to[k]) for k in range(2)]
    rep_copies = [remote(rep_out.at[k], rep_in.at[k], 7 + k, source[k]) for k in range(5)]
    ret_copies = [remote(ret_out.at[k], ret_in.at[k], 12 + k, to[k]) for k in range(2)]

    class Sum:
        def __init__(self, base, size, first, mine, second, sems):
            self.base, self.rows = base, size // n_dom
            self.first, self.mine, self.second, self.sems = first, mine, second, sems
            self.stages = (
                first.at[pl.ds(0, n_dom - 1)],
                second.at[pl.ds(0, n_grp - 1)],
                grads_ref.at[pl.ds(base, (n_dom - 1) * self.rows), :],
            )

        def copy(self, src, dst, stage, peer):
            return pltpu.make_async_remote_copy(
                src_ref=src,
                dst_ref=dst,
                send_sem=sum_send.at[self.sems + stage],
                recv_sem=sum_recv.at[self.sems + stage],
                device_id=peer,
                device_id_type=MESH,
            )

        def wait(self, sems, stage):
            whole = self.stages[stage]
            pltpu.make_async_copy(whole, whole, sems.at[self.sems + stage]).wait()

        def cut(self, index):
            return pl.ds(pl.multiple_of(self.base + index * self.rows, 8), self.rows)

        def start_scatter(self):
            def step(t, carry):
                peer = lax.rem(me + t, n_dom)
                self.copy(
                    part_ref.at[self.cut(peer), :], self.first.at[me], 0, (grp, peer)
                ).start()
                return carry

            lax.fori_loop(1, n_dom, step, 0)
            self.first[me] = part_ref[self.cut(me), :]

        def start_across(self):
            self.wait(sum_recv, 0)
            total = self.first[0]
            for t in range(1, n_dom):
                total += self.first[t]
            self.mine[...] = total

            def step(t, carry):
                peer = lax.rem(grp + t, n_grp)
                self.copy(self.mine, self.second.at[grp], 1, (peer, me)).start()
                return carry

            lax.fori_loop(1, n_grp, step, 0)
            self.second[grp] = total

        def start_gather(self):
            self.wait(sum_recv, 1)
            total = self.second[0]
            for t in range(1, n_grp):
                total += self.second[t]
            grads_ref[self.cut(me), :] = total
            mine = grads_ref.at[self.cut(me), :]

            def step(t, carry):
                peer = lax.rem(me + t, n_dom)
                self.copy(mine, mine, 2, (grp, peer)).start()
                return carry

            lax.fori_loop(1, n_dom, step, 0)

        def finish(self):
            for stage in range(3):
                self.wait(sum_send, stage)
            self.wait(sum_recv, 2)

    sum_a = Sum(2 * width, 4 * width, first_a, mine_a, second_a, 0)
    sum_b = Sum(0, 2 * width, first_b, mine_b, second_b, 3)

    for i in (11, 10):
        loads[i].wait()
    send_rows = [send_ref[pl.ds(t, 1), :] for t in to]
    listed = jnp.concatenate(
        send_rows + [rim_ref[1:2, :], rim_ref[0:1, :], jnp.zeros((1, sends), jnp.int32)], axis=0
    )
    listed_cols = listed.T
    sent = coarse + 5 * sends
    for k in range(5):
        hots[coarse + k * sends : coarse + (k + 1) * sends, :] = in_columns(
            listed_cols[:, k : k + 1], fine
        )
    loads[1].wait()
    for k in range(5):
        cot_out[k] = dot(
            hots[coarse + k * sends : coarse + (k + 1) * sends, :], cot_ref[...]
        ).astype(BF16)
    pl.semaphore_wait(barrier, n_dom + n_grp - 2)
    for k in (4, 2, 3, 0, 1):
        cot_copies[k].start()
    loads[0].wait()
    for k in range(2):
        hots[sent + k * rim : sent + (k + 1) * rim, :] = in_columns(
            listed_cols[:, 5 + k : 6 + k], fine
        )
    chosen = dot(hots[sent:, :], hidden_ref[...]).astype(BF16)
    for k in range(2):
        rim_out[k] = chosen[k * rim : (k + 1) * rim]
    for copy in rim_copies:
        copy.start()
    for i in range(NAMES):
        if i not in (0, 1, 10, 11):
            loads[i].wait()
    member_rows = [member_ref[pl.ds(s, 1), :] for s in source]

    for t in range(fine // 128):
        hots[0:coarse, t * 128 : (t + 1) * 128] = in_rows(own_ref[t : t + 1, :], coarse)
    far_hot = jnp.concatenate([in_rows(row, coarse) for row in member_rows], axis=1)
    own_pull = dot(
        hots[0:coarse, :], jnp.concatenate([cot_ref[...], jnp.ones((fine, width), BF16)], axis=1)
    )

    coarse_rows = coarse_ref[...]
    coarse_self = 0.5 * dot(coarse_rows, cws_ref[...])
    coarse_peer = jnp.concatenate(split(0.5 * dot(coarse_rows, cwp_ref[...])), axis=1)
    links = cnbrs_ref[...]
    link_cols = links.T
    coarse_slopes = []
    coarse_pool = jnp.zeros((coarse, width), F32)
    for j in range(slots):
        col = link_cols[:, j : j + 1]
        got = dot(in_columns(col, coarse), coarse_peer)
        bias = jnp.where(col == coarse, OFF, 0.0)
        act, slope = gate(coarse_self + got[:, :width] + (got[:, width:] + bias))
        coarse_pool += act
        coarse_slopes.append(slope)
    coarse_pool = coarse_pool.astype(BF16)
    link_hot = jnp.concatenate([in_rows(links[j : j + 1, :], coarse) for j in range(slots)], axis=1)

    for copy in cot_copies:
        copy.wait()
    arrived = cot_in[...].reshape(5 * sends, width)
    far_pull = dot(
        far_hot, jnp.concatenate([arrived, jnp.ones((5 * sends, width), BF16)], axis=1)
    )
    gathered = own_pull + far_pull
    pulled = gathered[:, :width]
    members = gathered[:, width:]
    pulled_b = pulled.astype(BF16)
    grad_pool = 0.5 * dot_nt(pulled_b, cwo_ref[...])
    grad_sum = jnp.zeros((coarse, width), F32)
    grad_pres = []
    for j in range(slots):
        grad_pre = grad_pool * coarse_slopes[j]
        grad_sum += grad_pre
        grad_pres.append(grad_pre.astype(BF16))
    grad_sum = grad_sum.astype(BF16)
    high, low = split(dot(link_hot, jnp.concatenate(grad_pres, axis=0)))
    node_grad = pulled + dot_nt(
        jnp.concatenate([grad_sum, high, low], axis=1),
        jnp.concatenate([cws_ref[...], cwp_ref[...], cwp_ref[...]], axis=1),
    )
    back = (node_grad / members).T.astype(BF16)
    replies = dot(back, far_hot).astype(BF16)
    for k in range(5):
        rep_out[k] = replies[:, k * sends : (k + 1) * sends]
    for copy in rep_copies:
        copy.start()
    part_ref[3 * width : 4 * width, :] = dot_tn(coarse_rows, grad_sum)
    part_ref[4 * width : 5 * width, :] = dot_tn(coarse_rows, high) + dot_tn(coarse_rows, low)
    part_ref[5 * width : 6 * width, :] = dot_tn(coarse_pool, pulled_b)

    self_turned = ws_ref[...].T
    peer_turned = wp_ref[...].T
    both_turned = jnp.concatenate([self_turned, peer_turned], axis=0)
    for t in range(fine // TILE):
        here = slice(t * TILE, (t + 1) * TILE)
        both = 0.5 * dot_nt(both_turned, hidden_ref[here, :])
        own_half[:, here] = both[:width]
        table_ref[t] = both[width:].astype(BF16)
        up_ref[:, here] = cot_ref[here, :].astype(F32).T

    for copy in rim_copies:
        copy.wait()
    lower = jnp.where(me > 0, 1.0, 0.0).astype(BF16)
    upper = jnp.where(me < n_dom - 1, 1.0, 0.0).astype(BF16)
    rims = jnp.concatenate([rim_in[0] * lower, rim_in[1] * upper], axis=0)
    for t in range(2 * rim // TILE):
        here = slice(t * TILE, (t + 1) * TILE)
        table_ref[fine // TILE + t] = (0.5 * dot_nt(peer_turned, rims[here])).astype(BF16)

    def places(b):
        first = pl.multiple_of(b * block, block)
        picked = nbrs_ref[:, pl.ds(first, block)]
        placed = jnp.where(picked < fine, picked - first, picked - (fine - block))
        return placed % TILE, placed // TILE

    def forward(b, carry):
        here = pl.ds(pl.multiple_of(b * block, block), block)
        near, far = places(b)
        table = jnp.concatenate(
            [table_ref[b * halves + t] for t in range(halves)]
            + [table_ref[fine // TILE + t] for t in range(2 * rim // TILE)],
            axis=0,
        )
        own = own_half[:, here]
        total = jnp.zeros((width, block), F32)
        for j in range(slots):
            got = dot(table, in_rows(near[j : j + 1, :], TILE))
            group = jnp.broadcast_to(far[j : j + 1, :], (width, block))
            peer = jnp.full((width, block), OFF, F32)
            for t in range(groups):
                peer = jnp.where(group == t, got[t * width : (t + 1) * width], peer)
            act, slope = gate(own + peer)
            total += act
            slope_ref[b, j] = slope
        pooled_ref[:, here] = total.astype(BF16)
        return carry

    lax.fori_loop(0, blocks, forward, 0)

    for copy in rep_copies:
        copy.wait()
    sources = jnp.concatenate([back] + [rep_in[k] for k in range(5)], axis=1)

    def arrive(b, carry):
        here = pl.ds(pl.multiple_of(b * block, block), block)
        up_ref[:, here] += dot(sources, hots[0:sent, here])
        return carry

    lax.fori_loop(0, blocks, arrive, 0)
    part_ref[2 * width : 3 * width, :] = dot_nt(pooled_ref[...], up_ref[...].astype(BF16))
    sum_a.start_scatter()
    rim_sum[...] = jnp.zeros((width, 2 * rim), F32)
    self_weight = ws_ref[...]
    peer_weight = wp_ref[...]
    out_weight = wo_ref[...]

    def backward(b, carry):
        first = pl.multiple_of(b * block, block)
        here = pl.ds(first, block)
        near, far = places(b)
        near_cols = near.T
        grad_pool = 0.5 * dot(out_weight, up_ref[:, here].astype(BF16))
        grad_sum = jnp.zeros((width, block), F32)
        peer_sum = jnp.zeros((groups * width, TILE), F32)
        for j in range(slots):
            grad_pre = grad_pool * slope_ref[b, j]
            grad_sum += grad_pre
            grad_b = grad_pre.astype(BF16)
            group = jnp.broadcast_to(far[j : j + 1, :].astype(jnp.int16), (width, block))
            zero = jnp.zeros((width, block), BF16)
            spread = jnp.concatenate(
                [jnp.where(group == t, grad_b, zero) for t in range(groups)], axis=0
            )
            peer_sum += dot(spread, in_columns(near_cols[:, j : j + 1], TILE))
        grad_ref[0:width, here] = grad_sum.astype(BF16)
        for t in range(halves):
            high, low = split(peer_sum[t * width : (t + 1) * width])
            cut = pl.ds(pl.multiple_of(first + t * TILE, TILE), TILE)
            grad_ref[width : 2 * width, cut] = high
            grad_ref[2 * width : 3 * width, cut] = low
        rim_sum[...] += jnp.concatenate(
            [peer_sum[t * width : (t + 1) * width] for t in range(halves, groups)], axis=1
        )
        return carry

    lax.fori_loop(0, blocks, backward, 0)

    high, low = split(rim_sum[...])
    turned = dot(grad_ref[...], hidden_ref[...])
    peer_grad = turned[width : 2 * width] + turned[2 * width :] + dot(high, rims) + dot(low, rims)
    part_ref[0:width, :] = turned[:width].T
    part_ref[width : 2 * width, :] = peer_grad.T
    sum_b.start_scatter()
    sum_a.start_across()
    rim_grad = (dot(peer_weight, high) + dot(peer_weight, low)).astype(BF16)
    ret_out[0] = rim_grad[:, rim:]
    ret_out[1] = rim_grad[:, :rim]
    for copy in ret_copies:
        copy.start()
    weights = jnp.concatenate([self_weight, peer_weight, peer_weight], axis=1)

    def own_part(b, carry):
        here = pl.ds(pl.multiple_of(b * block, block), block)
        up_ref[:, here] += dot(weights, grad_ref[:, here])
        return carry

    lax.fori_loop(0, blocks, own_part, 0)
    sum_b.start_across()
    sum_a.start_gather()
    for copy in ret_copies:
        copy.wait()
    returned = jnp.concatenate([ret_in[1] * upper, ret_in[0] * lower], axis=1)

    def give_back(b, carry):
        here = pl.ds(pl.multiple_of(b * block, block), block)
        out_ref[here, :] = (up_ref[:, here] + dot(returned, hots[sent:, here])).T
        return carry

    lax.fori_loop(0, blocks, give_back, 0)
    sum_b.start_gather()
    sum_a.finish()
    sum_b.finish()


def finish_kernel(node_ref, sums_ref, out_ref, *rest):
    parts, sem = rest[:-1], rest[-1]
    width = sums_ref.shape[1]
    copies = [pltpu.make_async_copy(node_ref, out_ref, sem.at[6])]
    for k, part in enumerate(parts):
        copies.append(
            pltpu.make_async_copy(sums_ref.at[pl.ds(k * width, width), :], part, sem.at[k])
        )
    for copy in copies:
        copy.start()
    for copy in copies:
        copy.wait()


def body(
    n_grp,
    n_dom,
    hidden_in,
    cotangent,
    coarse_state,
    edge_self,
    edge_peer,
    edge_out,
    coarse_self,
    coarse_peer,
    coarse_out,
    fine_nbrs,
    rim_rows,
    send_lists,
    member_slots,
    own_slots,
    coarse_nbrs,
):
    fine, width = hidden_in.shape
    coarse = coarse_state.shape[0]
    slots = fine_nbrs.shape[1]
    rim = rim_rows.shape[0] // 2
    sends = send_lists.shape[1]
    block = min(512, fine)
    blocks = fine // block
    vmem = pl.BlockSpec(memory_space=pltpu.VMEM)
    anywhere = pl.BlockSpec(memory_space=pl.ANY)
    args = (
        hidden_in,
        cotangent,
        coarse_state,
        edge_self,
        edge_peer,
        edge_out,
        coarse_self,
        coarse_peer,
        coarse_out,
        fine_nbrs.T,
        rim_rows.reshape(2, rim),
        send_lists,
        member_slots,
        own_slots.reshape(fine // 128, 128),
        coarse_nbrs.T,
    )
    node_grad, sums = pl.pallas_call(
        functools.partial(block_kernel, n_grp, n_dom),
        out_shape=(
            jax.ShapeDtypeStruct((fine, width), F32),
            jax.ShapeDtypeStruct((6 * width, width), F32),
        ),
        in_specs=[anywhere] * NAMES,
        out_specs=(vmem, vmem),
        scratch_shapes=[pltpu.VMEM(a.shape, a.dtype) for a in args]
        + [pltpu.VMEM((5, sends, width), BF16)] * 4
        + [pltpu.VMEM((2, rim, width), BF16)] * 4
        + [
            pltpu.VMEM((coarse + 5 * sends + 2 * rim, fine), BF16),
            pltpu.VMEM(((fine + 2 * rim) // TILE, width, TILE), BF16),
            pltpu.VMEM((width, fine), F32),
            pltpu.VMEM((blocks, slots, width, block), F32),
            pltpu.VMEM((width, fine), BF16),
            pltpu.VMEM((width, fine), F32),
            pltpu.VMEM((3 * width, fine), BF16),
            pltpu.VMEM((width, 2 * rim), F32),
            pltpu.VMEM((6 * width, width), F32),
            pltpu.VMEM((n_dom, 4 * width // n_dom, width), F32),
            pltpu.VMEM((n_dom, 2 * width // n_dom, width), F32),
            pltpu.VMEM((4 * width // n_dom, width), F32),
            pltpu.VMEM((2 * width // n_dom, width), F32),
            pltpu.VMEM((n_grp, 4 * width // n_dom, width), F32),
            pltpu.VMEM((n_grp, 2 * width // n_dom, width), F32),
            pltpu.SemaphoreType.DMA((NAMES,)),
            pltpu.SemaphoreType.DMA((14,)),
            pltpu.SemaphoreType.DMA((14,)),
            pltpu.SemaphoreType.DMA((6,)),
            pltpu.SemaphoreType.DMA((6,)),
        ],
        compiler_params=pltpu.CompilerParams(
            collective_id=0, has_side_effects=True, vmem_limit_bytes=56 * 1024 * 1024
        ),
        name="block",
    )(*args)
    square = jax.ShapeDtypeStruct((width, width), F32)
    return pl.pallas_call(
        finish_kernel,
        out_shape=(jax.ShapeDtypeStruct((fine, width), F32),) + (square,) * 6,
        in_specs=[vmem] * 2,
        out_specs=(anywhere,) * 7,
        scratch_shapes=[pltpu.SemaphoreType.DMA((7,))],
        name="finish",
    )(node_grad, sums)


def solution(mesh):
    rows = P(("grp", "dom"), None)
    flat = P(("grp", "dom"))
    whole = P()
    in_specs = (rows,) * 3 + (whole,) * 6 + (rows, flat, rows, rows, flat, rows)
    out_specs = (rows,) + (whole,) * 6
    return jax.shard_map(
        functools.partial(body, mesh.shape["grp"], mesh.shape["dom"]),
        mesh=mesh,
        in_specs=in_specs,
        out_specs=out_specs,
        check_vma=False,
    )
```

```python
import functools

import jax
import jax.numpy as jnp
from jax import lax
from jax.experimental import pallas as pl
from jax.experimental.pallas import tpu as pltpu
from jax.sharding import PartitionSpec as P

MESH = pl.DeviceIdType.MESH
F32 = jnp.float32
BF16 = jnp.bfloat16
OFF = -1.0e4
TILE = 256


def dot(a, b):
    return jnp.dot(a, b, preferred_element_type=F32)


def dot_nt(a, b):
    return lax.dot_general(a, b, (((1,), (1,)), ((), ())), preferred_element_type=F32)


def dot_tn(a, b):
    return lax.dot_general(a, b, (((0,), (0,)), ((), ())), preferred_element_type=F32)


def one_hot(index, shape, axis):
    ids = lax.broadcasted_iota(jnp.int32, shape, axis).astype(jnp.int16)
    hit = jnp.broadcast_to(index.astype(jnp.int16), shape) == ids
    return jnp.where(hit, jnp.ones(shape, BF16), jnp.zeros(shape, BF16))


def in_columns(index, width):
    return one_hot(index, (index.shape[0], width), 1)


def in_rows(index, height):
    return one_hot(index, (height, index.shape[1]), 0)


def split(values):
    high = values.astype(BF16)
    return high, (values - high.astype(F32)).astype(BF16)


def gate(half):
    tilt = jnp.tanh(half)
    both = 1.0 + tilt
    act = half * both
    return act, both + act * (2.0 - both)


NAMES = 15


def block_kernel(n_grp, n_dom, *refs):
    inputs = refs[:NAMES]
    out_ref, grads_ref = refs[NAMES : NAMES + 2]
    held = refs[NAMES + 2 : 2 * NAMES + 2]
    (
        cot_out,
        cot_in,
        rep_out,
        rep_in,
        rim_out,
        rim_in,
        ret_out,
        ret_in,
        hots,
        table_ref,
        own_half,
        slope_ref,
        pooled_ref,
        up_ref,
        grad_ref,
        rim_sum,
        part_ref,
        first_a,
        first_b,
        mine_a,
        mine_b,
        second_a,
        second_b,
        done_a,
        done_b,
        turned_out,
        load_sem,
        send_sem,
        recv_sem,
        sum_send,
        sum_recv,
        write_sem,
    ) = refs[2 * NAMES + 2 :]
    (
        hidden_ref,
        cot_ref,
        coarse_ref,
        ws_ref,
        wp_ref,
        wo_ref,
        cws_ref,
        cwp_ref,
        cwo_ref,
        nbrs_ref,
        rim_ref,
        send_ref,
        member_ref,
        own_ref,
        cnbrs_ref,
    ) = held
    loads = [
        pltpu.make_async_copy(src, dst, load_sem.at[i])
        for i, (src, dst) in enumerate(zip(inputs, held))
    ]
    grp = lax.axis_index("grp")
    me = lax.axis_index("dom")
    fine, width = hidden_ref.shape
    coarse = coarse_ref.shape[0]
    slots = nbrs_ref.shape[0]
    rim = rim_ref.shape[1]
    sends = send_ref.shape[1]
    block = min(512, fine)
    blocks = fine // block
    halves = block // TILE
    groups = halves + 2 * rim // TILE
    offsets = (1, -1, 2, -2, n_dom // 2)
    to = [lax.rem(me + (n_dom + o), n_dom) for o in offsets]
    source = [lax.rem(me + (n_dom - o), n_dom) for o in offsets]

    barrier = pltpu.get_barrier_semaphore()

    for peer in to:
        pl.semaphore_signal(barrier, inc=1, device_id=(grp, peer), device_id_type=MESH)
    order = (11, 1, 10, 0, 12, 13, 2, 6, 7, 8, 14, 3, 4, 5, 9)
    for i in order:
        loads[i].start()

    def greet_dom(t, carry):
        peer = (grp, lax.rem(me + t, n_dom))
        pl.semaphore_signal(barrier, inc=1, device_id=peer, device_id_type=MESH)
        return carry

    def greet_grp(t, carry):
        peer = (lax.rem(grp + t, n_grp), me)
        pl.semaphore_signal(barrier, inc=1, device_id=peer, device_id_type=MESH)
        return carry

    lax.fori_loop(3, n_dom // 2, greet_dom, 0, unroll=True)
    lax.fori_loop(n_dom // 2 + 1, n_dom - 2, greet_dom, 0, unroll=True)
    lax.fori_loop(1, n_grp, greet_grp, 0, unroll=True)

    def remote(src, dst, index, peer):
        return pltpu.make_async_remote_copy(
            src_ref=src,
            dst_ref=dst,
            send_sem=send_sem.at[index],
            recv_sem=recv_sem.at[index],
            device_id=(grp, peer),
            device_id_type=MESH,
        )

    cot_copies = [remote(cot_out.at[k], cot_in.at[k], k, to[k]) for k in range(5)]
    rim_copies = [remote(rim_out.at[k], rim_in.at[k], 5 + k, to[k]) for k in range(2)]
    rep_copies = [remote(rep_out.at[k], rep_in.at[k], 7 + k, source[k]) for k in range(5)]
    ret_copies = [remote(ret_out.at[k], ret_in.at[k], 12 + k, to[k]) for k in range(2)]

    def hops(t):
        along_y = n_dom // 4
        x, y = t / along_y, (t % along_y) / 2
        return min(x, 4 - x) + min(y, along_y / 2 - y)

    dom_order = sorted(range(1, n_dom), key=hops, reverse=True)
    grp_order = sorted(range(1, n_grp), key=lambda t: -min(t, n_grp - t))

    class Sum:
        def __init__(self, base, size, first, mine, second, done, sems):
            self.base, self.rows = base, size // n_dom
            self.first, self.mine, self.second = first, mine, second
            self.done, self.sems = done, sems
            self.keep = pltpu.make_async_copy(
                done, grads_ref.at[self.cut(me), :], write_sem.at[sems // 3]
            )
            self.stages = (
                first.at[pl.ds(0, n_dom - 1)],
                second.at[pl.ds(0, n_grp - 1)],
                grads_ref.at[pl.ds(base, (n_dom - 1) * self.rows), :],
            )

        def copy(self, src, dst, stage, peer):
            return pltpu.make_async_remote_copy(
                src_ref=src,
                dst_ref=dst,
                send_sem=sum_send.at[self.sems + stage],
                recv_sem=sum_recv.at[self.sems + stage],
                device_id=peer,
                device_id_type=MESH,
            )

        def wait(self, sems, stage):
            whole = self.stages[stage]
            pltpu.make_async_copy(whole, whole, sems.at[self.sems + stage]).wait()

        def cut(self, index):
            return pl.ds(pl.multiple_of(self.base + index * self.rows, 8), self.rows)

        def start_scatter(self):
            for t in dom_order:
                peer = lax.rem(me + t, n_dom)
                self.copy(
                    part_ref.at[self.cut(peer), :], self.first.at[me], 0, (grp, peer)
                ).start()
            self.first[me] = part_ref[self.cut(me), :]

        def start_across(self):
            self.wait(sum_recv, 0)
            total = self.first[0]
            for t in range(1, n_dom):
                total += self.first[t]
            self.mine[...] = total
            for t in grp_order:
                peer = lax.rem(grp + t, n_grp)
                self.copy(self.mine, self.second.at[grp], 1, (peer, me)).start()
            self.second[grp] = total

        def start_gather(self):
            self.wait(sum_recv, 1)
            total = self.second[0]
            for t in range(1, n_grp):
                total += self.second[t]
            self.done[...] = total
            place = grads_ref.at[self.cut(me), :]
            for t in dom_order:
                peer = lax.rem(me + t, n_dom)
                self.copy(self.done, place, 2, (grp, peer)).start()
            self.keep.start()

        def finish(self):
            for stage in range(3):
                self.wait(sum_send, stage)
            self.wait(sum_recv, 2)
            self.keep.wait()

    sum_a = Sum(2 * width, 4 * width, first_a, mine_a, second_a, done_a, 0)
    sum_b = Sum(0, 2 * width, first_b, mine_b, second_b, done_b, 3)

    for i in (11, 10):
        loads[i].wait()
    send_rows = [send_ref[pl.ds(t, 1), :] for t in to]
    listed = jnp.concatenate(
        send_rows + [rim_ref[1:2, :], rim_ref[0:1, :], jnp.zeros((1, sends), jnp.int32)], axis=0
    )
    listed_cols = listed.T
    sent = coarse + 5 * sends
    for k in range(5):
        hots[coarse + k * sends : coarse + (k + 1) * sends, :] = in_columns(
            listed_cols[:, k : k + 1], fine
        )
    loads[1].wait()
    for k in range(5):
        cot_out[k] = dot(
            hots[coarse + k * sends : coarse + (k + 1) * sends, :], cot_ref[...]
        ).astype(BF16)
    pl.semaphore_wait(barrier, n_dom + n_grp - 2)
    for k in (4, 2, 3, 0, 1):
        cot_copies[k].start()
    loads[0].wait()
    for k in range(2):
        hots[sent + k * rim : sent + (k + 1) * rim, :] = in_columns(
            listed_cols[:, 5 + k : 6 + k], fine
        )
    chosen = dot(hots[sent:, :], hidden_ref[...]).astype(BF16)
    for k in range(2):
        rim_out[k] = chosen[k * rim : (k + 1) * rim]
    for copy in rim_copies:
        copy.start()
    for i in range(NAMES):
        if i not in (0, 1, 10, 11):
            loads[i].wait()
    member_rows = [member_ref[pl.ds(s, 1), :] for s in source]

    for t in range(fine // 128):
        hots[0:coarse, t * 128 : (t + 1) * 128] = in_rows(own_ref[t : t + 1, :], coarse)
    far_hot = jnp.concatenate([in_rows(row, coarse) for row in member_rows], axis=1)
    own_pull = dot(hots[0:coarse, :], cot_ref[...])
    members = dot(hots[0:coarse, :], jnp.ones((fine, width), BF16)) + dot(
        far_hot, jnp.ones((5 * sends, width), BF16)
    )
    share = 1.0 / members
    out_turned = (0.5 * cwo_ref[...].astype(F32)).T.astype(BF16)
    peer_turned = cwp_ref[...].T
    all_turned = jnp.concatenate([cws_ref[...].T, peer_turned, peer_turned], axis=0)

    coarse_rows = coarse_ref[...]
    coarse_self = 0.5 * dot(coarse_rows, cws_ref[...])
    coarse_peer = jnp.concatenate(split(0.5 * dot(coarse_rows, cwp_ref[...])), axis=1)
    links = cnbrs_ref[...]
    link_cols = links.T
    coarse_slopes = []
    coarse_pool = jnp.zeros((coarse, width), F32)
    for j in range(slots):
        col = link_cols[:, j : j + 1]
        got = dot(in_columns(col, coarse), coarse_peer)
        bias = jnp.where(col == coarse, OFF, 0.0)
        act, slope = gate(coarse_self + got[:, :width] + (got[:, width:] + bias))
        coarse_pool += act
        coarse_slopes.append(slope)
    coarse_pool = coarse_pool.astype(BF16)
    link_hot = jnp.concatenate([in_rows(links[j : j + 1, :], coarse) for j in range(slots)], axis=1)

    for copy in cot_copies:
        copy.wait_recv()
    arrived = cot_in[...].reshape(5 * sends, width)
    pulled = own_pull + dot(far_hot, arrived)
    pulled_b = pulled.astype(BF16)
    grad_pool = dot(pulled_b, out_turned)
    grad_sum = jnp.zeros((coarse, width), F32)
    grad_pres = []
    for j in range(slots):
        grad_pre = grad_pool * coarse_slopes[j]
        grad_sum += grad_pre
        grad_pres.append(grad_pre.astype(BF16))
    grad_sum = grad_sum.astype(BF16)
    high, low = split(dot(link_hot, jnp.concatenate(grad_pres, axis=0)))
    node_grad = pulled + dot(jnp.concatenate([grad_sum, high, low], axis=1), all_turned)
    back = (node_grad * share).T.astype(BF16)
    replies = dot(back, far_hot).astype(BF16)
    for k in range(5):
        rep_out[k] = replies[:, k * sends : (k + 1) * sends]
    for copy in rep_copies:
        copy.start()
    part_ref[3 * width : 4 * width, :] = dot_tn(coarse_rows, grad_sum)
    part_ref[4 * width : 5 * width, :] = dot_tn(coarse_rows, high) + dot_tn(coarse_rows, low)
    part_ref[5 * width : 6 * width, :] = dot_tn(coarse_pool, pulled_b)

    self_turned = ws_ref[...].T
    peer_turned = wp_ref[...].T
    both_turned = jnp.concatenate([self_turned, peer_turned], axis=0)
    for t in range(fine // TILE):
        here = slice(t * TILE, (t + 1) * TILE)
        both = 0.5 * dot_nt(both_turned, hidden_ref[here, :])
        own_half[:, here] = both[:width]
        table_ref[t] = both[width:].astype(BF16)
        up_ref[:, here] = cot_ref[here, :].astype(F32).T

    for copy in rim_copies:
        copy.wait_recv()
    lower = jnp.where(me > 0, 1.0, 0.0).astype(BF16)
    upper = jnp.where(me < n_dom - 1, 1.0, 0.0).astype(BF16)
    rims = jnp.concatenate([rim_in[0] * lower, rim_in[1] * upper], axis=0)
    for t in range(2 * rim // TILE):
        here = slice(t * TILE, (t + 1) * TILE)
        table_ref[fine // TILE + t] = (0.5 * dot_nt(peer_turned, rims[here])).astype(BF16)

    def places(b):
        first = pl.multiple_of(b * block, block)
        picked = nbrs_ref[:, pl.ds(first, block)]
        placed = jnp.where(picked < fine, picked - first, picked - (fine - block))
        return placed % TILE, placed // TILE

    def forward(b, carry):
        here = pl.ds(pl.multiple_of(b * block, block), block)
        near, far = places(b)
        table = jnp.concatenate(
            [table_ref[b * halves + t] for t in range(halves)]
            + [table_ref[fine // TILE + t] for t in range(2 * rim // TILE)],
            axis=0,
        )
        own = own_half[:, here]
        total = jnp.zeros((width, block), F32)
        for j in range(slots):
            got = dot(table, in_rows(near[j : j + 1, :], TILE))
            group = jnp.broadcast_to(far[j : j + 1, :], (width, block))
            peer = jnp.full((width, block), OFF, F32)
            for t in range(groups):
                peer = jnp.where(group == t, got[t * width : (t + 1) * width], peer)
            act, slope = gate(own + peer)
            total += act
            slope_ref[b, j] = slope
        pooled_ref[:, here] = total.astype(BF16)
        return carry

    lax.fori_loop(0, blocks, forward, 0)

    for copy in rep_copies:
        copy.wait_recv()
    sources = jnp.concatenate([back] + [rep_in[k] for k in range(5)], axis=1)

    def arrive(b, carry):
        here = pl.ds(pl.multiple_of(b * block, block), block)
        up_ref[:, here] += dot(sources, hots[0:sent, here])
        return carry

    lax.fori_loop(0, blocks, arrive, 0)
    part_ref[2 * width : 3 * width, :] = dot_nt(pooled_ref[...], up_ref[...].astype(BF16))
    sum_a.start_scatter()
    rim_sum[...] = jnp.zeros((width, 2 * rim), F32)
    self_weight = ws_ref[...]
    peer_weight = wp_ref[...]
    out_weight = wo_ref[...]

    def backward(b, carry):
        first = pl.multiple_of(b * block, block)
        here = pl.ds(first, block)
        near, far = places(b)
        near_cols = near.T
        grad_pool = 0.5 * dot(out_weight, up_ref[:, here].astype(BF16))
        peer_sum = jnp.zeros((groups * width, TILE), F32)
        for c in range(block // TILE):
            lo = c * TILE
            total = jnp.zeros((width, TILE), F32)
            left, right = [], []
            for j in range(slots):
                grad_pre = grad_pool[:, lo : lo + TILE] * slope_ref[b, j, :, lo : lo + TILE]
                total += grad_pre
                grad_b = grad_pre.astype(BF16)
                group = jnp.broadcast_to(
                    far[j : j + 1, lo : lo + TILE].astype(jnp.int16), (width, TILE)
                )
                zero = jnp.zeros((width, TILE), BF16)
                left.append(
                    jnp.concatenate([jnp.where(group == t, grad_b, zero) for t in range(groups)], axis=0)
                )
                right.append(in_columns(near_cols[lo : lo + TILE, j : j + 1], TILE))
            peer_sum += dot(jnp.concatenate(left, axis=1), jnp.concatenate(right, axis=0))
            cut = pl.ds(pl.multiple_of(first + lo, TILE), TILE)
            grad_ref[0:width, cut] = total.astype(BF16)
        for t in range(halves):
            high, low = split(peer_sum[t * width : (t + 1) * width])
            cut = pl.ds(pl.multiple_of(first + t * TILE, TILE), TILE)
            grad_ref[width : 2 * width, cut] = high
            grad_ref[2 * width : 3 * width, cut] = low
        rim_sum[...] += jnp.concatenate(
            [peer_sum[t * width : (t + 1) * width] for t in range(halves, groups)], axis=1
        )
        return carry

    lax.fori_loop(0, blocks, backward, 0)

    high, low = split(rim_sum[...])
    turned = dot(grad_ref[...], hidden_ref[...])
    peer_grad = turned[width : 2 * width] + turned[2 * width :] + dot(high, rims) + dot(low, rims)
    part_ref[0:width, :] = turned[:width].T
    part_ref[width : 2 * width, :] = peer_grad.T
    sum_b.start_scatter()
    sum_a.start_across()
    rim_grad = (dot(peer_weight, high) + dot(peer_weight, low)).astype(BF16)
    ret_out[0] = rim_grad[:, rim:]
    ret_out[1] = rim_grad[:, :rim]
    for copy in ret_copies:
        copy.start()
    weights = jnp.concatenate([self_weight, peer_weight, peer_weight], axis=1)

    def own_part(b, carry):
        here = pl.ds(pl.multiple_of(b * block, block), block)
        up_ref[:, here] += dot(weights, grad_ref[:, here])
        return carry

    lax.fori_loop(0, blocks, own_part, 0)
    sum_b.start_across()
    sum_a.start_gather()
    sum_b.start_gather()
    for copy in ret_copies:
        copy.wait_recv()
    returned = jnp.concatenate([ret_in[1] * upper, ret_in[0] * lower], axis=1)

    def give_back(b, carry):
        here = pl.ds(pl.multiple_of(b * block, block), block)
        turned_out[here, :] = (up_ref[:, here] + dot(returned, hots[sent:, here])).T
        write(b).start()
        return carry

    def write(b):
        here = pl.ds(pl.multiple_of(b * block, block), block)
        return pltpu.make_async_copy(
            turned_out.at[here, :], out_ref.at[here, :], write_sem.at[2 + b]
        )

    lax.fori_loop(0, blocks, give_back, 0)
    for copy in cot_copies + rim_copies + rep_copies + ret_copies:
        copy.wait_send()
    for b in range(blocks):
        write(b).wait()
    sum_a.finish()
    sum_b.finish()


def finish_kernel(node_ref, sums_ref, out_ref, *rest):
    parts, sem = rest[:-1], rest[-1]
    width = sums_ref.shape[1]
    copies = [pltpu.make_async_copy(node_ref, out_ref, sem.at[6])]
    for k, part in enumerate(parts):
        copies.append(
            pltpu.make_async_copy(sums_ref.at[pl.ds(k * width, width), :], part, sem.at[k])
        )
    for copy in copies:
        copy.start()
    for copy in copies:
        copy.wait()


def body(
    n_grp,
    n_dom,
    hidden_in,
    cotangent,
    coarse_state,
    edge_self,
    edge_peer,
    edge_out,
    coarse_self,
    coarse_peer,
    coarse_out,
    fine_nbrs,
    rim_rows,
    send_lists,
    member_slots,
    own_slots,
    coarse_nbrs,
):
    fine, width = hidden_in.shape
    coarse = coarse_state.shape[0]
    slots = fine_nbrs.shape[1]
    rim = rim_rows.shape[0] // 2
    sends = send_lists.shape[1]
    block = min(512, fine)
    blocks = fine // block
    vmem = pl.BlockSpec(memory_space=pltpu.VMEM)
    anywhere = pl.BlockSpec(memory_space=pl.ANY)
    args = (
        hidden_in,
        cotangent,
        coarse_state,
        edge_self,
        edge_peer,
        edge_out,
        coarse_self,
        coarse_peer,
        coarse_out,
        fine_nbrs.T,
        rim_rows.reshape(2, rim),
        send_lists,
        member_slots,
        own_slots.reshape(fine // 128, 128),
        coarse_nbrs.T,
    )
    node_grad, sums = pl.pallas_call(
        functools.partial(block_kernel, n_grp, n_dom),
        out_shape=(
            jax.ShapeDtypeStruct((fine, width), F32),
            jax.ShapeDtypeStruct((6 * width, width), F32),
        ),
        in_specs=[anywhere] * NAMES,
        out_specs=(anywhere, anywhere),
        scratch_shapes=[pltpu.VMEM(a.shape, a.dtype) for a in args]
        + [pltpu.VMEM((5, sends, width), BF16)] * 4
        + [pltpu.VMEM((2, rim, width), BF16)] * 4
        + [
            pltpu.VMEM((coarse + 5 * sends + 2 * rim, fine), BF16),
            pltpu.VMEM(((fine + 2 * rim) // TILE, width, TILE), BF16),
            pltpu.VMEM((width, fine), F32),
            pltpu.VMEM((blocks, slots, width, block), F32),
            pltpu.VMEM((width, fine), BF16),
            pltpu.VMEM((width, fine), F32),
            pltpu.VMEM((3 * width, fine), BF16),
            pltpu.VMEM((width, 2 * rim), F32),
            pltpu.VMEM((6 * width, width), F32),
            pltpu.VMEM((n_dom, 4 * width // n_dom, width), F32),
            pltpu.VMEM((n_dom, 2 * width // n_dom, width), F32),
            pltpu.VMEM((4 * width // n_dom, width), F32),
            pltpu.VMEM((2 * width // n_dom, width), F32),
            pltpu.VMEM((n_grp, 4 * width // n_dom, width), F32),
            pltpu.VMEM((n_grp, 2 * width // n_dom, width), F32),
            pltpu.VMEM((4 * width // n_dom, width), F32),
            pltpu.VMEM((2 * width // n_dom, width), F32),
            pltpu.VMEM((fine, width), F32),
            pltpu.SemaphoreType.DMA((NAMES,)),
            pltpu.SemaphoreType.DMA((14,)),
            pltpu.SemaphoreType.DMA((14,)),
            pltpu.SemaphoreType.DMA((6,)),
            pltpu.SemaphoreType.DMA((6,)),
            pltpu.SemaphoreType.DMA((2 + blocks,)),
        ],
        compiler_params=pltpu.CompilerParams(
            collective_id=0, has_side_effects=True, vmem_limit_bytes=56 * 1024 * 1024
        ),
        name="block",
    )(*args)
    square = jax.ShapeDtypeStruct((width, width), F32)
    return pl.pallas_call(
        finish_kernel,
        out_shape=(jax.ShapeDtypeStruct((fine, width), F32),) + (square,) * 6,
        in_specs=[vmem] * 2,
        out_specs=(anywhere,) * 7,
        scratch_shapes=[pltpu.SemaphoreType.DMA((7,))],
        name="finish",
    )(node_grad, sums)


def solution(mesh):
    rows = P(("grp", "dom"), None)
    flat = P(("grp", "dom"))
    whole = P()
    in_specs = (rows,) * 3 + (whole,) * 6 + (rows, flat, rows, rows, flat, rows)
    out_specs = (rows,) + (whole,) * 6
    return jax.shard_map(
        functools.partial(body, mesh.shape["grp"], mesh.shape["dom"]),
        mesh=mesh,
        in_specs=in_specs,
        out_specs=out_specs,
        check_vma=False,
    )
```

```python
import functools

import jax
import jax.numpy as jnp
from jax import lax
from jax.experimental import pallas as pl
from jax.experimental.pallas import tpu as pltpu
from jax.sharding import PartitionSpec as P

MESH = pl.DeviceIdType.MESH
F32 = jnp.float32
BF16 = jnp.bfloat16
OFF = -1.0e4
TILE = 256
CUTS = 4


def dot(a, b):
    return jnp.dot(a, b, preferred_element_type=F32)


def dot_nt(a, b):
    return lax.dot_general(a, b, (((1,), (1,)), ((), ())), preferred_element_type=F32)


def dot_tn(a, b):
    return lax.dot_general(a, b, (((0,), (0,)), ((), ())), preferred_element_type=F32)


def one_hot(index, shape, axis):
    ids = lax.broadcasted_iota(jnp.int32, shape, axis).astype(jnp.int16)
    hit = jnp.broadcast_to(index.astype(jnp.int16), shape) == ids
    return jnp.where(hit, jnp.ones(shape, BF16), jnp.zeros(shape, BF16))


def in_columns(index, width):
    return one_hot(index, (index.shape[0], width), 1)


def in_rows(index, height):
    return one_hot(index, (height, index.shape[1]), 0)


def split(values):
    high = values.astype(BF16)
    return high, (values - high.astype(F32)).astype(BF16)


def gate(half):
    tilt = jnp.tanh(half)
    both = 1.0 + tilt
    act = half * both
    return act, both + act * (2.0 - both)


NAMES = 15


def block_kernel(n_grp, n_dom, *refs):
    inputs = refs[:NAMES]
    out_ref, grads_ref = refs[NAMES : NAMES + 2]
    held = refs[NAMES + 2 : 2 * NAMES + 2]
    (
        cot_out,
        cot_in,
        rep_out,
        rep_in,
        rim_out,
        rim_in,
        ret_out,
        ret_in,
        hots,
        table_ref,
        own_half,
        slope_ref,
        pooled_ref,
        up_ref,
        grad_ref,
        rim_sum,
        part_ref,
        first_a,
        first_b,
        mine_a,
        mine_b,
        second_a,
        second_b,
        done_a,
        done_b,
        turned_out,
        load_sem,
        send_sem,
        recv_sem,
        sum_send,
        sum_recv,
        write_sem,
    ) = refs[2 * NAMES + 2 :]
    (
        hidden_ref,
        cot_ref,
        coarse_ref,
        ws_ref,
        wp_ref,
        wo_ref,
        cws_ref,
        cwp_ref,
        cwo_ref,
        nbrs_ref,
        rim_ref,
        send_ref,
        member_ref,
        own_ref,
        cnbrs_ref,
    ) = held
    loads = [
        pltpu.make_async_copy(src, dst, load_sem.at[i])
        for i, (src, dst) in enumerate(zip(inputs, held))
    ]
    grp = lax.axis_index("grp")
    me = lax.axis_index("dom")
    fine, width = hidden_ref.shape
    coarse = coarse_ref.shape[0]
    slots = nbrs_ref.shape[0]
    rim = rim_ref.shape[1]
    sends = send_ref.shape[1]
    block = min(512, fine)
    blocks = fine // block
    halves = block // TILE
    groups = halves + 2 * rim // TILE
    offsets = (1, -1, 2, -2, n_dom // 2)
    to = [lax.rem(me + (n_dom + o), n_dom) for o in offsets]
    source = [lax.rem(me + (n_dom - o), n_dom) for o in offsets]

    barrier = pltpu.get_barrier_semaphore()

    for peer in to:
        pl.semaphore_signal(barrier, inc=1, device_id=(grp, peer), device_id_type=MESH)
    order = (11, 1, 10, 0, 12, 13, 2, 6, 7, 8, 14, 3, 4, 5, 9)
    for i in order:
        loads[i].start()

    def greet_dom(t, carry):
        peer = (grp, lax.rem(me + t, n_dom))
        pl.semaphore_signal(barrier, inc=1, device_id=peer, device_id_type=MESH)
        return carry

    def greet_grp(t, carry):
        peer = (lax.rem(grp + t, n_grp), me)
        pl.semaphore_signal(barrier, inc=1, device_id=peer, device_id_type=MESH)
        return carry

    lax.fori_loop(3, n_dom // 2, greet_dom, 0, unroll=True)
    lax.fori_loop(n_dom // 2 + 1, n_dom - 2, greet_dom, 0, unroll=True)
    lax.fori_loop(1, n_grp, greet_grp, 0, unroll=True)

    def remote(src, dst, index, peer):
        return pltpu.make_async_remote_copy(
            src_ref=src,
            dst_ref=dst,
            send_sem=send_sem.at[index],
            recv_sem=recv_sem.at[index],
            device_id=(grp, peer),
            device_id_type=MESH,
        )

    cot_copies = [remote(cot_out.at[k], cot_in.at[k], k, to[k]) for k in range(5)]
    rim_copies = [remote(rim_out.at[k], rim_in.at[k], 5 + k, to[k]) for k in range(2)]
    rep_copies = [remote(rep_out.at[k], rep_in.at[k], 7 + k, source[k]) for k in range(5)]
    ret_copies = [remote(ret_out.at[k], ret_in.at[k], 12 + k, to[k]) for k in range(2)]

    def hops(t):
        along_y = n_dom // 4
        x, y = t / along_y, (t % along_y) / 2
        return min(x, 4 - x) + min(y, along_y / 2 - y)

    dom_order = sorted(range(1, n_dom), key=hops, reverse=True)
    grp_order = sorted(range(1, n_grp), key=lambda t: -min(t, n_grp - t))

    class Sum:
        def __init__(self, base, size, first, mine, second, done, sems):
            self.base, self.rows = base, size // n_dom
            self.first, self.mine, self.second = first, mine, second
            self.done, self.sems = done, sems
            self.keep = pltpu.make_async_copy(
                done, grads_ref.at[self.cut(me), :], write_sem.at[sems // 3]
            )
            self.stages = (
                first.at[pl.ds(0, n_dom - 1)],
                second.at[pl.ds(0, n_grp - 1)],
                grads_ref.at[pl.ds(base, (n_dom - 1) * self.rows), :],
            )

        def copy(self, src, dst, stage, peer):
            return pltpu.make_async_remote_copy(
                src_ref=src,
                dst_ref=dst,
                send_sem=sum_send.at[self.sems + stage],
                recv_sem=sum_recv.at[self.sems + stage],
                device_id=peer,
                device_id_type=MESH,
            )

        def wait(self, sems, stage):
            whole = self.stages[stage]
            pltpu.make_async_copy(whole, whole, sems.at[self.sems + stage]).wait()

        def cut(self, index):
            return pl.ds(pl.multiple_of(self.base + index * self.rows, 8), self.rows)

        def start_scatter(self):
            for t in dom_order:
                peer = lax.rem(me + t, n_dom)
                self.copy(
                    part_ref.at[self.cut(peer), :], self.first.at[me], 0, (grp, peer)
                ).start()
            self.first[me] = part_ref[self.cut(me), :]

        def start_across(self):
            self.wait(sum_recv, 0)
            total = self.first[0]
            for t in range(1, n_dom):
                total += self.first[t]
            self.mine[...] = total
            for t in grp_order:
                peer = lax.rem(grp + t, n_grp)
                self.copy(self.mine, self.second.at[grp], 1, (peer, me)).start()
            self.second[grp] = total

        def start_gather(self):
            self.wait(sum_recv, 1)
            total = self.second[0]
            for t in range(1, n_grp):
                total += self.second[t]
            self.done[...] = total
            place = grads_ref.at[self.cut(me), :]
            for t in dom_order:
                peer = lax.rem(me + t, n_dom)
                self.copy(self.done, place, 2, (grp, peer)).start()
            self.keep.start()

        def finish(self):
            for stage in range(3):
                self.wait(sum_send, stage)
            self.wait(sum_recv, 2)
            self.keep.wait()

    sum_a = Sum(2 * width, 4 * width, first_a, mine_a, second_a, done_a, 0)
    sum_b = Sum(0, 2 * width, first_b, mine_b, second_b, done_b, 3)

    for i in (11, 10):
        loads[i].wait()
    send_rows = [send_ref[pl.ds(t, 1), :] for t in to]
    listed = jnp.concatenate(
        send_rows + [rim_ref[1:2, :], rim_ref[0:1, :], jnp.zeros((1, sends), jnp.int32)], axis=0
    )
    listed_cols = listed.T
    sent = coarse + 5 * sends
    for k in range(5):
        hots[coarse + k * sends : coarse + (k + 1) * sends, :] = in_columns(
            listed_cols[:, k : k + 1], fine
        )
    loads[1].wait()
    for k in range(5):
        cot_out[k] = dot(
            hots[coarse + k * sends : coarse + (k + 1) * sends, :], cot_ref[...]
        ).astype(BF16)
    pl.semaphore_wait(barrier, n_dom + n_grp - 2)
    for k in (4, 2, 3, 0, 1):
        cot_copies[k].start()
    loads[0].wait()
    for k in range(2):
        hots[sent + k * rim : sent + (k + 1) * rim, :] = in_columns(
            listed_cols[:, 5 + k : 6 + k], fine
        )
    chosen = dot(hots[sent:, :], hidden_ref[...]).astype(BF16)
    for k in range(2):
        rim_out[k] = chosen[k * rim : (k + 1) * rim]
    for copy in rim_copies:
        copy.start()
    for i in range(NAMES):
        if i not in (0, 1, 10, 11):
            loads[i].wait()
    member_rows = [member_ref[pl.ds(s, 1), :] for s in source]

    for t in range(fine // 128):
        hots[0:coarse, t * 128 : (t + 1) * 128] = in_rows(own_ref[t : t + 1, :], coarse)
    far_hot = jnp.concatenate([in_rows(row, coarse) for row in member_rows], axis=1)
    own_pull = dot(hots[0:coarse, :], cot_ref[...])
    members = dot(hots[0:coarse, :], jnp.ones((fine, width), BF16)) + dot(
        far_hot, jnp.ones((5 * sends, width), BF16)
    )
    share = 1.0 / members
    out_turned = (0.5 * cwo_ref[...].astype(F32)).T.astype(BF16)
    peer_turned = cwp_ref[...].T
    all_turned = jnp.concatenate([cws_ref[...].T, peer_turned, peer_turned], axis=0)

    coarse_rows = coarse_ref[...]
    coarse_self = 0.5 * dot(coarse_rows, cws_ref[...])
    coarse_peer = jnp.concatenate(split(0.5 * dot(coarse_rows, cwp_ref[...])), axis=1)
    links = cnbrs_ref[...]
    link_cols = links.T
    coarse_slopes = []
    coarse_pool = jnp.zeros((coarse, width), F32)
    for j in range(slots):
        col = link_cols[:, j : j + 1]
        got = dot(in_columns(col, coarse), coarse_peer)
        bias = jnp.where(col == coarse, OFF, 0.0)
        act, slope = gate(coarse_self + got[:, :width] + (got[:, width:] + bias))
        coarse_pool += act
        coarse_slopes.append(slope)
    coarse_pool = coarse_pool.astype(BF16)
    link_hot = jnp.concatenate([in_rows(links[j : j + 1, :], coarse) for j in range(slots)], axis=1)

    self_turned = ws_ref[...].T
    peer_turned = wp_ref[...].T
    both_turned = jnp.concatenate([self_turned, peer_turned], axis=0)
    for t in range(fine // TILE):
        here = slice(t * TILE, (t + 1) * TILE)
        both = 0.5 * dot_nt(both_turned, hidden_ref[here, :])
        own_half[:, here] = both[:width]
        table_ref[t] = both[width:].astype(BF16)
        up_ref[:, here] = cot_ref[here, :].astype(F32).T

    for copy in cot_copies:
        copy.wait_recv()
    arrived = cot_in[...].reshape(5 * sends, width)
    pulled = own_pull + dot(far_hot, arrived)
    pulled_b = pulled.astype(BF16)
    grad_pool = dot(pulled_b, out_turned)
    grad_sum = jnp.zeros((coarse, width), F32)
    grad_pres = []
    for j in range(slots):
        grad_pre = grad_pool * coarse_slopes[j]
        grad_sum += grad_pre
        grad_pres.append(grad_pre.astype(BF16))
    grad_sum = grad_sum.astype(BF16)
    high, low = split(dot(link_hot, jnp.concatenate(grad_pres, axis=0)))
    node_grad = pulled + dot(jnp.concatenate([grad_sum, high, low], axis=1), all_turned)
    back = (node_grad * share).T.astype(BF16)
    replies = dot(back, far_hot).astype(BF16)
    for k in range(5):
        rep_out[k] = replies[:, k * sends : (k + 1) * sends]
    for copy in rep_copies:
        copy.start()
    part_ref[3 * width : 4 * width, :] = dot_tn(coarse_rows, grad_sum)
    part_ref[4 * width : 5 * width, :] = dot_tn(coarse_rows, high) + dot_tn(coarse_rows, low)
    part_ref[5 * width : 6 * width, :] = dot_tn(coarse_pool, pulled_b)

    for copy in rim_copies:
        copy.wait_recv()
    lower = jnp.where(me > 0, 1.0, 0.0).astype(BF16)
    upper = jnp.where(me < n_dom - 1, 1.0, 0.0).astype(BF16)
    rims = jnp.concatenate([rim_in[0] * lower, rim_in[1] * upper], axis=0)
    for t in range(2 * rim // TILE):
        here = slice(t * TILE, (t + 1) * TILE)
        table_ref[fine // TILE + t] = (0.5 * dot_nt(peer_turned, rims[here])).astype(BF16)

    def places(b):
        first = pl.multiple_of(b * block, block)
        picked = nbrs_ref[:, pl.ds(first, block)]
        placed = jnp.where(picked < fine, picked - first, picked - (fine - block))
        return placed % TILE, placed // TILE

    def forward(b, carry):
        here = pl.ds(pl.multiple_of(b * block, block), block)
        near, far = places(b)
        table = jnp.concatenate(
            [table_ref[b * halves + t] for t in range(halves)]
            + [table_ref[fine // TILE + t] for t in range(2 * rim // TILE)],
            axis=0,
        )
        own = own_half[:, here]
        total = jnp.zeros((width, block), F32)
        for j in range(slots):
            got = dot(table, in_rows(near[j : j + 1, :], TILE))
            group = jnp.broadcast_to(far[j : j + 1, :], (width, block))
            peer = jnp.full((width, block), OFF, F32)
            for t in range(groups):
                peer = jnp.where(group == t, got[t * width : (t + 1) * width], peer)
            act, slope = gate(own + peer)
            total += act
            slope_ref[b, j] = slope
        pooled_ref[:, here] = total.astype(BF16)
        return carry

    lax.fori_loop(0, blocks, forward, 0)

    for copy in rep_copies:
        copy.wait_recv()
    sources = jnp.concatenate([back] + [rep_in[k] for k in range(5)], axis=1)

    def arrive(b, carry):
        here = pl.ds(pl.multiple_of(b * block, block), block)
        up_ref[:, here] += dot(sources, hots[0:sent, here])
        return carry

    lax.fori_loop(0, blocks, arrive, 0)
    part_ref[2 * width : 3 * width, :] = dot_nt(pooled_ref[...], up_ref[...].astype(BF16))
    sum_a.start_scatter()
    rim_sum[...] = jnp.zeros((width, 2 * rim), F32)
    self_weight = ws_ref[...]
    peer_weight = wp_ref[...]
    out_weight = wo_ref[...]

    def backward(b, carry):
        first = pl.multiple_of(b * block, block)
        here = pl.ds(first, block)
        near, far = places(b)
        near_cols = near.T
        grad_pool = 0.5 * dot(out_weight, up_ref[:, here].astype(BF16))
        peer_sum = jnp.zeros((groups * width, TILE), F32)
        for c in range(block // TILE):
            lo = c * TILE
            total = jnp.zeros((width, TILE), F32)
            left, right = [], []
            for j in range(slots):
                grad_pre = grad_pool[:, lo : lo + TILE] * slope_ref[b, j, :, lo : lo + TILE]
                total += grad_pre
                grad_b = grad_pre.astype(BF16)
                group = jnp.broadcast_to(
                    far[j : j + 1, lo : lo + TILE].astype(jnp.int16), (width, TILE)
                )
                zero = jnp.zeros((width, TILE), BF16)
                left.append(
                    jnp.concatenate([jnp.where(group == t, grad_b, zero) for t in range(groups)], axis=0)
                )
                right.append(in_columns(near_cols[lo : lo + TILE, j : j + 1], TILE))
            peer_sum += dot(jnp.concatenate(left, axis=1), jnp.concatenate(right, axis=0))
            cut = pl.ds(pl.multiple_of(first + lo, TILE), TILE)
            grad_ref[0:width, cut] = total.astype(BF16)
        for t in range(halves):
            high, low = split(peer_sum[t * width : (t + 1) * width])
            cut = pl.ds(pl.multiple_of(first + t * TILE, TILE), TILE)
            grad_ref[width : 2 * width, cut] = high
            grad_ref[2 * width : 3 * width, cut] = low
        rim_sum[...] += jnp.concatenate(
            [peer_sum[t * width : (t + 1) * width] for t in range(halves, groups)], axis=1
        )
        return carry

    lax.fori_loop(0, blocks, backward, 0)

    high, low = split(rim_sum[...])
    turned = dot(grad_ref[...], hidden_ref[...])
    peer_grad = turned[width : 2 * width] + turned[2 * width :] + dot(high, rims) + dot(low, rims)
    part_ref[0:width, :] = turned[:width].T
    part_ref[width : 2 * width, :] = peer_grad.T
    sum_b.start_scatter()
    sum_a.start_across()
    rim_grad = (dot(peer_weight, high) + dot(peer_weight, low)).astype(BF16)
    ret_out[0] = rim_grad[:, rim:]
    ret_out[1] = rim_grad[:, :rim]
    for copy in ret_copies:
        copy.start()
    weights = jnp.concatenate([self_weight, peer_weight, peer_weight], axis=1)

    def own_part(b, carry):
        here = pl.ds(pl.multiple_of(b * block, block), block)
        up_ref[:, here] += dot(weights, grad_ref[:, here])
        return carry

    lax.fori_loop(0, blocks, own_part, 0)
    sum_b.start_across()
    sum_a.start_gather()
    sum_b.start_gather()
    for copy in ret_copies:
        copy.wait_recv()
    returned = jnp.concatenate([ret_in[1] * upper, ret_in[0] * lower], axis=1)

    def give_back(b, carry):
        here = pl.ds(pl.multiple_of(b * block, block), block)
        turned_out[here, :] = (up_ref[:, here] + dot(returned, hots[sent:, here])).T
        write(b).start()
        return carry

    def write(b):
        here = pl.ds(pl.multiple_of(b * block, block), block)
        return pltpu.make_async_copy(
            turned_out.at[here, :], out_ref.at[here, :], write_sem.at[2 + b]
        )

    lax.fori_loop(0, blocks, give_back, 0)
    for copy in cot_copies + rim_copies + rep_copies + ret_copies:
        copy.wait_send()
    for b in range(blocks):
        write(b).wait()
    sum_a.finish()
    sum_b.finish()


def finish_kernel(node_ref, sums_ref, out_ref, *rest):
    parts, (node_held, sums_held, load_sem, sem) = rest[:6], rest[6:]
    width = sums_ref.shape[1]
    size = node_ref.shape[0] // CUTS
    moves = []
    for t in range(CUTS):
        here = pl.ds(t * size, size)
        moves.append((node_ref.at[here, :], node_held.at[here, :], out_ref.at[here, :]))
    for k, part in enumerate(parts):
        here = pl.ds(k * width, width)
        moves.append((sums_ref.at[here, :], sums_held.at[here, :], part))
    loads = [
        pltpu.make_async_copy(src, held, load_sem.at[i]) for i, (src, held, _) in enumerate(moves)
    ]
    writes = [
        pltpu.make_async_copy(held, dst, sem.at[i]) for i, (_, held, dst) in enumerate(moves)
    ]
    for load in loads:
        load.start()
    for load, write in zip(loads, writes):
        load.wait()
        write.start()
    for write in writes:
        write.wait()


def body(
    n_grp,
    n_dom,
    hidden_in,
    cotangent,
    coarse_state,
    edge_self,
    edge_peer,
    edge_out,
    coarse_self,
    coarse_peer,
    coarse_out,
    fine_nbrs,
    rim_rows,
    send_lists,
    member_slots,
    own_slots,
    coarse_nbrs,
):
    fine, width = hidden_in.shape
    coarse = coarse_state.shape[0]
    slots = fine_nbrs.shape[1]
    rim = rim_rows.shape[0] // 2
    sends = send_lists.shape[1]
    block = min(512, fine)
    blocks = fine // block
    vmem = pl.BlockSpec(memory_space=pltpu.VMEM)
    anywhere = pl.BlockSpec(memory_space=pl.ANY)
    args = (
        hidden_in,
        cotangent,
        coarse_state,
        edge_self,
        edge_peer,
        edge_out,
        coarse_self,
        coarse_peer,
        coarse_out,
        fine_nbrs.T,
        rim_rows.reshape(2, rim),
        send_lists,
        member_slots,
        own_slots.reshape(fine // 128, 128),
        coarse_nbrs.T,
    )
    node_grad, sums = pl.pallas_call(
        functools.partial(block_kernel, n_grp, n_dom),
        out_shape=(
            jax.ShapeDtypeStruct((fine, width), F32),
            jax.ShapeDtypeStruct((6 * width, width), F32),
        ),
        in_specs=[anywhere] * NAMES,
        out_specs=(anywhere, anywhere),
        scratch_shapes=[pltpu.VMEM(a.shape, a.dtype) for a in args]
        + [pltpu.VMEM((5, sends, width), BF16)] * 4
        + [pltpu.VMEM((2, rim, width), BF16)] * 4
        + [
            pltpu.VMEM((coarse + 5 * sends + 2 * rim, fine), BF16),
            pltpu.VMEM(((fine + 2 * rim) // TILE, width, TILE), BF16),
            pltpu.VMEM((width, fine), F32),
            pltpu.VMEM((blocks, slots, width, block), F32),
            pltpu.VMEM((width, fine), BF16),
            pltpu.VMEM((width, fine), F32),
            pltpu.VMEM((3 * width, fine), BF16),
            pltpu.VMEM((width, 2 * rim), F32),
            pltpu.VMEM((6 * width, width), F32),
            pltpu.VMEM((n_dom, 4 * width // n_dom, width), F32),
            pltpu.VMEM((n_dom, 2 * width // n_dom, width), F32),
            pltpu.VMEM((4 * width // n_dom, width), F32),
            pltpu.VMEM((2 * width // n_dom, width), F32),
            pltpu.VMEM((n_grp, 4 * width // n_dom, width), F32),
            pltpu.VMEM((n_grp, 2 * width // n_dom, width), F32),
            pltpu.VMEM((4 * width // n_dom, width), F32),
            pltpu.VMEM((2 * width // n_dom, width), F32),
            pltpu.VMEM((fine, width), F32),
            pltpu.SemaphoreType.DMA((NAMES,)),
            pltpu.SemaphoreType.DMA((14,)),
            pltpu.SemaphoreType.DMA((14,)),
            pltpu.SemaphoreType.DMA((6,)),
            pltpu.SemaphoreType.DMA((6,)),
            pltpu.SemaphoreType.DMA((2 + blocks,)),
        ],
        compiler_params=pltpu.CompilerParams(
            collective_id=0, has_side_effects=True, vmem_limit_bytes=56 * 1024 * 1024
        ),
        name="block",
    )(*args)
    square = jax.ShapeDtypeStruct((width, width), F32)
    return pl.pallas_call(
        finish_kernel,
        out_shape=(jax.ShapeDtypeStruct((fine, width), F32),) + (square,) * 6,
        in_specs=[anywhere] * 2,
        out_specs=(anywhere,) * 7,
        scratch_shapes=[
            pltpu.VMEM((fine, width), F32),
            pltpu.VMEM((6 * width, width), F32),
            pltpu.SemaphoreType.DMA((6 + CUTS,)),
            pltpu.SemaphoreType.DMA((6 + CUTS,)),
        ],
        compiler_params=pltpu.CompilerParams(vmem_limit_bytes=56 * 1024 * 1024),
        name="finish",
    )(node_grad, sums)


def solution(mesh):
    rows = P(("grp", "dom"), None)
    flat = P(("grp", "dom"))
    whole = P()
    in_specs = (rows,) * 3 + (whole,) * 6 + (rows, flat, rows, rows, flat, rows)
    out_specs = (rows,) + (whole,) * 6
    return jax.shard_map(
        functools.partial(body, mesh.shape["grp"], mesh.shape["dom"]),
        mesh=mesh,
        in_specs=in_specs,
        out_specs=out_specs,
        check_vma=False,
    )
```

```python
import functools

import jax
import jax.numpy as jnp
from jax import lax
from jax.experimental import pallas as pl
from jax.experimental.pallas import tpu as pltpu
from jax.sharding import PartitionSpec as P

MESH = pl.DeviceIdType.MESH
F32 = jnp.float32
BF16 = jnp.bfloat16
OFF = -1.0e4
TILE = 256
CUTS = 4


def dot(a, b):
    return jnp.dot(a, b, preferred_element_type=F32)


def dot_nt(a, b):
    return lax.dot_general(a, b, (((1,), (1,)), ((), ())), preferred_element_type=F32)


def dot_tn(a, b):
    return lax.dot_general(a, b, (((0,), (0,)), ((), ())), preferred_element_type=F32)


def one_hot(index, shape, axis):
    ids = lax.broadcasted_iota(jnp.int32, shape, axis).astype(jnp.int16)
    hit = jnp.broadcast_to(index.astype(jnp.int16), shape) == ids
    return jnp.where(hit, jnp.ones(shape, BF16), jnp.zeros(shape, BF16))


def in_columns(index, width):
    return one_hot(index, (index.shape[0], width), 1)


def in_rows(index, height):
    return one_hot(index, (height, index.shape[1]), 0)


def split(values):
    high = values.astype(BF16)
    return high, (values - high.astype(F32)).astype(BF16)


def gate(half):
    tilt = jnp.tanh(half)
    both = 1.0 + tilt
    act = half * both
    return act, both + act * (2.0 - both)


NAMES = 15


def block_kernel(n_grp, n_dom, *refs):
    inputs = refs[:NAMES]
    out_ref, grads_ref = refs[NAMES : NAMES + 2]
    held = refs[NAMES + 2 : 2 * NAMES + 2]
    (
        cot_out,
        cot_in,
        rep_out,
        rep_in,
        rim_out,
        rim_in,
        ret_out,
        ret_in,
        hots,
        table_ref,
        own_half,
        slope_ref,
        pooled_ref,
        up_ref,
        grad_ref,
        rim_sum,
        part_ref,
        first_a,
        first_b,
        mine_a,
        mine_b,
        second_a,
        second_b,
        done_a,
        done_b,
        turned_out,
        load_sem,
        send_sem,
        recv_sem,
        sum_send,
        sum_recv,
        write_sem,
    ) = refs[2 * NAMES + 2 :]
    (
        hidden_ref,
        cot_ref,
        coarse_ref,
        ws_ref,
        wp_ref,
        wo_ref,
        cws_ref,
        cwp_ref,
        cwo_ref,
        nbrs_ref,
        rim_ref,
        send_ref,
        member_ref,
        own_ref,
        cnbrs_ref,
    ) = held
    loads = [
        pltpu.make_async_copy(src, dst, load_sem.at[i])
        for i, (src, dst) in enumerate(zip(inputs, held))
    ]
    grp = lax.axis_index("grp")
    me = lax.axis_index("dom")
    fine, width = hidden_ref.shape
    coarse = coarse_ref.shape[0]
    slots = nbrs_ref.shape[0]
    rim = rim_ref.shape[1]
    sends = send_ref.shape[1]
    block = min(512, fine)
    blocks = fine // block
    halves = block // TILE
    groups = halves + 2 * rim // TILE
    offsets = (1, -1, 2, -2, n_dom // 2)
    to = [lax.rem(me + (n_dom + o), n_dom) for o in offsets]
    source = [lax.rem(me + (n_dom - o), n_dom) for o in offsets]

    barrier = pltpu.get_barrier_semaphore()

    for peer in to:
        pl.semaphore_signal(barrier, inc=1, device_id=(grp, peer), device_id_type=MESH)
    order = (11, 1, 10, 0, 12, 13, 2, 6, 7, 8, 14, 3, 4, 5, 9)
    for i in order:
        loads[i].start()

    def greet_dom(t, carry):
        peer = (grp, lax.rem(me + t, n_dom))
        pl.semaphore_signal(barrier, inc=1, device_id=peer, device_id_type=MESH)
        return carry

    def greet_grp(t, carry):
        peer = (lax.rem(grp + t, n_grp), me)
        pl.semaphore_signal(barrier, inc=1, device_id=peer, device_id_type=MESH)
        return carry

    lax.fori_loop(3, n_dom // 2, greet_dom, 0, unroll=True)
    lax.fori_loop(n_dom // 2 + 1, n_dom - 2, greet_dom, 0, unroll=True)
    lax.fori_loop(1, n_grp, greet_grp, 0, unroll=True)

    def remote(src, dst, index, peer):
        return pltpu.make_async_remote_copy(
            src_ref=src,
            dst_ref=dst,
            send_sem=send_sem.at[index],
            recv_sem=recv_sem.at[index],
            device_id=(grp, peer),
            device_id_type=MESH,
        )

    cot_copies = [remote(cot_out.at[k], cot_in.at[k], k, to[k]) for k in range(5)]
    rim_copies = [remote(rim_out.at[k], rim_in.at[k], 5 + k, to[k]) for k in range(2)]
    rep_copies = [remote(rep_out.at[k], rep_in.at[k], 7 + k, source[k]) for k in range(5)]
    ret_copies = [remote(ret_out.at[k], ret_in.at[k], 12 + k, to[k]) for k in range(2)]

    def hops(t):
        along_y = n_dom // 4
        x, y = t / along_y, (t % along_y) / 2
        return min(x, 4 - x) + min(y, along_y / 2 - y)

    dom_order = sorted(range(1, n_dom), key=hops, reverse=True)
    grp_order = sorted(range(1, n_grp), key=lambda t: -min(t, n_grp - t))

    class Sum:
        def __init__(self, base, size, first, mine, second, done, sems):
            self.base, self.rows = base, size // n_dom
            self.first, self.mine, self.second = first, mine, second
            self.done, self.sems = done, sems
            self.keep = pltpu.make_async_copy(
                done, grads_ref.at[self.cut(me), :], write_sem.at[sems // 3]
            )
            self.stages = (
                first.at[pl.ds(0, n_dom - 1)],
                second.at[pl.ds(0, n_grp - 1)],
                grads_ref.at[pl.ds(base, (n_dom - 1) * self.rows), :],
            )

        def copy(self, src, dst, stage, peer):
            return pltpu.make_async_remote_copy(
                src_ref=src,
                dst_ref=dst,
                send_sem=sum_send.at[self.sems + stage],
                recv_sem=sum_recv.at[self.sems + stage],
                device_id=peer,
                device_id_type=MESH,
            )

        def wait(self, sems, stage):
            whole = self.stages[stage]
            pltpu.make_async_copy(whole, whole, sems.at[self.sems + stage]).wait()

        def cut(self, index):
            return pl.ds(pl.multiple_of(self.base + index * self.rows, 8), self.rows)

        def start_scatter(self):
            for t in dom_order:
                peer = lax.rem(me + t, n_dom)
                self.copy(
                    part_ref.at[self.cut(peer), :], self.first.at[me], 0, (grp, peer)
                ).start()
            self.first[me] = part_ref[self.cut(me), :]

        def start_across(self):
            self.wait(sum_recv, 0)
            total = self.first[0]
            for t in range(1, n_dom):
                total += self.first[t]
            self.mine[...] = total
            for t in grp_order:
                peer = lax.rem(grp + t, n_grp)
                self.copy(self.mine, self.second.at[grp], 1, (peer, me)).start()
            self.second[grp] = total

        def start_gather(self):
            self.wait(sum_recv, 1)
            total = self.second[0]
            for t in range(1, n_grp):
                total += self.second[t]
            self.done[...] = total
            place = grads_ref.at[self.cut(me), :]
            for t in dom_order:
                peer = lax.rem(me + t, n_dom)
                self.copy(self.done, place, 2, (grp, peer)).start()
            self.keep.start()

        def finish(self):
            for stage in range(3):
                self.wait(sum_send, stage)
            self.wait(sum_recv, 2)
            self.keep.wait()

    sum_a = Sum(2 * width, 4 * width, first_a, mine_a, second_a, done_a, 0)
    sum_b = Sum(0, 2 * width, first_b, mine_b, second_b, done_b, 3)

    for i in (11, 10):
        loads[i].wait()
    send_rows = [send_ref[pl.ds(t, 1), :] for t in to]
    listed = jnp.concatenate(
        send_rows + [rim_ref[1:2, :], rim_ref[0:1, :], jnp.zeros((1, sends), jnp.int32)], axis=0
    )
    listed_cols = listed.T
    sent = coarse + 5 * sends
    for k in range(5):
        hots[coarse + k * sends : coarse + (k + 1) * sends, :] = in_columns(
            listed_cols[:, k : k + 1], fine
        )
    loads[1].wait()
    for k in range(5):
        cot_out[k] = dot(
            hots[coarse + k * sends : coarse + (k + 1) * sends, :], cot_ref[...]
        ).astype(BF16)
    pl.semaphore_wait(barrier, n_dom + n_grp - 2)
    for k in (4, 2, 3, 0, 1):
        cot_copies[k].start()
    loads[0].wait()
    for k in range(2):
        hots[sent + k * rim : sent + (k + 1) * rim, :] = in_columns(
            listed_cols[:, 5 + k : 6 + k], fine
        )
    chosen = dot(hots[sent:, :], hidden_ref[...]).astype(BF16)
    for k in range(2):
        rim_out[k] = chosen[k * rim : (k + 1) * rim]
    for copy in rim_copies:
        copy.start()
    for i in range(NAMES):
        if i not in (0, 1, 10, 11):
            loads[i].wait()
    member_rows = [member_ref[pl.ds(s, 1), :] for s in source]

    for t in range(fine // 128):
        hots[0:coarse, t * 128 : (t + 1) * 128] = in_rows(own_ref[t : t + 1, :], coarse)
    far_hot = jnp.concatenate([in_rows(row, coarse) for row in member_rows], axis=1)
    own_pull = dot(hots[0:coarse, :], cot_ref[...])
    members = dot(hots[0:coarse, :], jnp.ones((fine, width), BF16)) + dot(
        far_hot, jnp.ones((5 * sends, width), BF16)
    )
    share = 1.0 / members
    out_turned = (0.5 * cwo_ref[...].astype(F32)).T.astype(BF16)
    peer_turned = cwp_ref[...].T
    all_turned = jnp.concatenate([cws_ref[...].T, peer_turned, peer_turned], axis=0)

    coarse_rows = coarse_ref[...]
    coarse_self = 0.5 * dot(coarse_rows, cws_ref[...])
    coarse_peer = jnp.concatenate(split(0.5 * dot(coarse_rows, cwp_ref[...])), axis=1)
    links = cnbrs_ref[...]
    link_cols = links.T
    coarse_slopes = []
    coarse_pool = jnp.zeros((coarse, width), F32)
    for j in range(slots):
        col = link_cols[:, j : j + 1]
        got = dot(in_columns(col, coarse), coarse_peer)
        bias = jnp.where(col == coarse, OFF, 0.0)
        act, slope = gate(coarse_self + got[:, :width] + (got[:, width:] + bias))
        coarse_pool += act
        coarse_slopes.append(slope)
    coarse_pool = coarse_pool.astype(BF16)
    link_hot = jnp.concatenate([in_rows(links[j : j + 1, :], coarse) for j in range(slots)], axis=1)

    self_turned = ws_ref[...].T
    peer_turned = wp_ref[...].T
    both_turned = jnp.concatenate([self_turned, peer_turned], axis=0)
    for t in range(fine // TILE):
        here = slice(t * TILE, (t + 1) * TILE)
        both = 0.5 * dot_nt(both_turned, hidden_ref[here, :])
        own_half[:, here] = both[:width]
        table_ref[t] = both[width:].astype(BF16)
        up_ref[:, here] = cot_ref[here, :].astype(F32).T

    for copy in cot_copies:
        copy.wait_recv()
    arrived = cot_in[...].reshape(5 * sends, width)
    pulled = own_pull + dot(far_hot, arrived)
    pulled_b = pulled.astype(BF16)
    grad_pool = dot(pulled_b, out_turned)
    grad_sum = jnp.zeros((coarse, width), F32)
    grad_pres = []
    for j in range(slots):
        grad_pre = grad_pool * coarse_slopes[j]
        grad_sum += grad_pre
        grad_pres.append(grad_pre.astype(BF16))
    grad_sum = grad_sum.astype(BF16)
    high, low = split(dot(link_hot, jnp.concatenate(grad_pres, axis=0)))
    node_grad = pulled + dot(jnp.concatenate([grad_sum, high, low], axis=1), all_turned)
    back = (node_grad * share).T.astype(BF16)
    replies = dot(back, far_hot).astype(BF16)
    for k in range(5):
        rep_out[k] = replies[:, k * sends : (k + 1) * sends]
    for copy in rep_copies:
        copy.start()
    part_ref[3 * width : 4 * width, :] = dot_tn(coarse_rows, grad_sum)
    part_ref[4 * width : 5 * width, :] = dot_tn(coarse_rows, high) + dot_tn(coarse_rows, low)
    part_ref[5 * width : 6 * width, :] = dot_tn(coarse_pool, pulled_b)

    for copy in rim_copies:
        copy.wait_recv()
    lower = jnp.where(me > 0, 1.0, 0.0).astype(BF16)
    upper = jnp.where(me < n_dom - 1, 1.0, 0.0).astype(BF16)
    rims = jnp.concatenate([rim_in[0] * lower, rim_in[1] * upper], axis=0)
    for t in range(2 * rim // TILE):
        here = slice(t * TILE, (t + 1) * TILE)
        table_ref[fine // TILE + t] = (0.5 * dot_nt(peer_turned, rims[here])).astype(BF16)

    def places(b):
        first = pl.multiple_of(b * block, block)
        picked = nbrs_ref[:, pl.ds(first, block)]
        placed = jnp.where(picked < fine, picked - first, picked - (fine - block))
        return placed % TILE, placed // TILE

    def forward(b, carry):
        here = pl.ds(pl.multiple_of(b * block, block), block)
        near, far = places(b)
        table = jnp.concatenate(
            [table_ref[b * halves + t] for t in range(halves)]
            + [table_ref[fine // TILE + t] for t in range(2 * rim // TILE)],
            axis=0,
        )
        own = own_half[:, here]
        total = jnp.zeros((width, block), F32)
        for j in range(slots):
            got = dot(table, in_rows(near[j : j + 1, :], TILE))
            group = jnp.broadcast_to(far[j : j + 1, :], (width, block))
            peer = jnp.full((width, block), OFF, F32)
            for t in range(groups):
                peer = jnp.where(group == t, got[t * width : (t + 1) * width], peer)
            act, slope = gate(own + peer)
            total += act
            slope_ref[b, j] = slope.astype(BF16)
        pooled_ref[:, here] = total.astype(BF16)
        return carry

    lax.fori_loop(0, blocks, forward, 0)

    for copy in rep_copies:
        copy.wait_recv()
    sources = jnp.concatenate([back] + [rep_in[k] for k in range(5)], axis=1)

    def arrive(b, carry):
        here = pl.ds(pl.multiple_of(b * block, block), block)
        up_ref[:, here] += dot(sources, hots[0:sent, here])
        return carry

    lax.fori_loop(0, blocks, arrive, 0)
    part_ref[2 * width : 3 * width, :] = dot_nt(pooled_ref[...], up_ref[...].astype(BF16))
    sum_a.start_scatter()
    rim_sum[...] = jnp.zeros((width, 2 * rim), F32)
    self_weight = ws_ref[...]
    peer_weight = wp_ref[...]
    out_weight = wo_ref[...]

    def backward(b, carry):
        first = pl.multiple_of(b * block, block)
        here = pl.ds(first, block)
        near, far = places(b)
        near_cols = near.T
        grad_pool = (0.5 * dot(out_weight, up_ref[:, here].astype(BF16))).astype(BF16)
        peer_sum = jnp.zeros((groups * width, TILE), F32)
        for c in range(block // TILE):
            lo = c * TILE
            total = jnp.zeros((width, TILE), F32)
            left, right = [], []
            for j in range(slots):
                grad_b = grad_pool[:, lo : lo + TILE] * slope_ref[b, j, :, lo : lo + TILE]
                total += grad_b.astype(F32)
                group = jnp.broadcast_to(
                    far[j : j + 1, lo : lo + TILE].astype(jnp.int16), (width, TILE)
                )
                zero = jnp.zeros((width, TILE), BF16)
                left.append(
                    jnp.concatenate([jnp.where(group == t, grad_b, zero) for t in range(groups)], axis=0)
                )
                right.append(in_columns(near_cols[lo : lo + TILE, j : j + 1], TILE))
            peer_sum += dot(jnp.concatenate(left, axis=1), jnp.concatenate(right, axis=0))
            cut = pl.ds(pl.multiple_of(first + lo, TILE), TILE)
            grad_ref[0:width, cut] = total.astype(BF16)
        for t in range(halves):
            high, low = split(peer_sum[t * width : (t + 1) * width])
            cut = pl.ds(pl.multiple_of(first + t * TILE, TILE), TILE)
            grad_ref[width : 2 * width, cut] = high
            grad_ref[2 * width : 3 * width, cut] = low
        rim_sum[...] += jnp.concatenate(
            [peer_sum[t * width : (t + 1) * width] for t in range(halves, groups)], axis=1
        )
        return carry

    lax.fori_loop(0, blocks, backward, 0)

    high, low = split(rim_sum[...])
    turned = dot(grad_ref[...], hidden_ref[...])
    peer_grad = turned[width : 2 * width] + turned[2 * width :] + dot(high, rims) + dot(low, rims)
    part_ref[0:width, :] = turned[:width].T
    part_ref[width : 2 * width, :] = peer_grad.T
    sum_b.start_scatter()
    sum_a.start_across()
    rim_grad = (dot(peer_weight, high) + dot(peer_weight, low)).astype(BF16)
    ret_out[0] = rim_grad[:, rim:]
    ret_out[1] = rim_grad[:, :rim]
    for copy in ret_copies:
        copy.start()
    weights = jnp.concatenate([self_weight, peer_weight, peer_weight], axis=1)

    def own_part(b, carry):
        here = pl.ds(pl.multiple_of(b * block, block), block)
        up_ref[:, here] += dot(weights, grad_ref[:, here])
        return carry

    lax.fori_loop(0, blocks, own_part, 0)
    sum_b.start_across()
    sum_a.start_gather()
    sum_b.start_gather()
    for copy in ret_copies:
        copy.wait_recv()
    returned = jnp.concatenate([ret_in[1] * upper, ret_in[0] * lower], axis=1)

    def give_back(b, carry):
        here = pl.ds(pl.multiple_of(b * block, block), block)
        turned_out[here, :] = (up_ref[:, here] + dot(returned, hots[sent:, here])).T
        write(b).start()
        return carry

    def write(b):
        here = pl.ds(pl.multiple_of(b * block, block), block)
        return pltpu.make_async_copy(
            turned_out.at[here, :], out_ref.at[here, :], write_sem.at[2 + b]
        )

    lax.fori_loop(0, blocks, give_back, 0)
    for copy in cot_copies + rim_copies + rep_copies + ret_copies:
        copy.wait_send()
    for b in range(blocks):
        write(b).wait()
    sum_a.finish()
    sum_b.finish()


def finish_kernel(node_ref, sums_ref, out_ref, *rest):
    parts, (node_held, sums_held, load_sem, sem) = rest[:6], rest[6:]
    width = sums_ref.shape[1]
    size = node_ref.shape[0] // CUTS
    moves = []
    for t in range(CUTS):
        here = pl.ds(t * size, size)
        moves.append((node_ref.at[here, :], node_held.at[here, :], out_ref.at[here, :]))
    for k, part in enumerate(parts):
        here = pl.ds(k * width, width)
        moves.append((sums_ref.at[here, :], sums_held.at[here, :], part))
    loads = [
        pltpu.make_async_copy(src, held, load_sem.at[i]) for i, (src, held, _) in enumerate(moves)
    ]
    writes = [
        pltpu.make_async_copy(held, dst, sem.at[i]) for i, (_, held, dst) in enumerate(moves)
    ]
    for load in loads:
        load.start()
    for load, write in zip(loads, writes):
        load.wait()
        write.start()
    for write in writes:
        write.wait()


def body(
    n_grp,
    n_dom,
    hidden_in,
    cotangent,
    coarse_state,
    edge_self,
    edge_peer,
    edge_out,
    coarse_self,
    coarse_peer,
    coarse_out,
    fine_nbrs,
    rim_rows,
    send_lists,
    member_slots,
    own_slots,
    coarse_nbrs,
):
    fine, width = hidden_in.shape
    coarse = coarse_state.shape[0]
    slots = fine_nbrs.shape[1]
    rim = rim_rows.shape[0] // 2
    sends = send_lists.shape[1]
    block = min(512, fine)
    blocks = fine // block
    vmem = pl.BlockSpec(memory_space=pltpu.VMEM)
    anywhere = pl.BlockSpec(memory_space=pl.ANY)
    args = (
        hidden_in,
        cotangent,
        coarse_state,
        edge_self,
        edge_peer,
        edge_out,
        coarse_self,
        coarse_peer,
        coarse_out,
        fine_nbrs.T,
        rim_rows.reshape(2, rim),
        send_lists,
        member_slots,
        own_slots.reshape(fine // 128, 128),
        coarse_nbrs.T,
    )
    node_grad, sums = pl.pallas_call(
        functools.partial(block_kernel, n_grp, n_dom),
        out_shape=(
            jax.ShapeDtypeStruct((fine, width), F32),
            jax.ShapeDtypeStruct((6 * width, width), F32),
        ),
        in_specs=[anywhere] * NAMES,
        out_specs=(anywhere, anywhere),
        scratch_shapes=[pltpu.VMEM(a.shape, a.dtype) for a in args]
        + [pltpu.VMEM((5, sends, width), BF16)] * 4
        + [pltpu.VMEM((2, rim, width), BF16)] * 4
        + [
            pltpu.VMEM((coarse + 5 * sends + 2 * rim, fine), BF16),
            pltpu.VMEM(((fine + 2 * rim) // TILE, width, TILE), BF16),
            pltpu.VMEM((width, fine), F32),
            pltpu.VMEM((blocks, slots, width, block), BF16),
            pltpu.VMEM((width, fine), BF16),
            pltpu.VMEM((width, fine), F32),
            pltpu.VMEM((3 * width, fine), BF16),
            pltpu.VMEM((width, 2 * rim), F32),
            pltpu.VMEM((6 * width, width), F32),
            pltpu.VMEM((n_dom, 4 * width // n_dom, width), F32),
            pltpu.VMEM((n_dom, 2 * width // n_dom, width), F32),
            pltpu.VMEM((4 * width // n_dom, width), F32),
            pltpu.VMEM((2 * width // n_dom, width), F32),
            pltpu.VMEM((n_grp, 4 * width // n_dom, width), F32),
            pltpu.VMEM((n_grp, 2 * width // n_dom, width), F32),
            pltpu.VMEM((4 * width // n_dom, width), F32),
            pltpu.VMEM((2 * width // n_dom, width), F32),
            pltpu.VMEM((fine, width), F32),
            pltpu.SemaphoreType.DMA((NAMES,)),
            pltpu.SemaphoreType.DMA((14,)),
            pltpu.SemaphoreType.DMA((14,)),
            pltpu.SemaphoreType.DMA((6,)),
            pltpu.SemaphoreType.DMA((6,)),
            pltpu.SemaphoreType.DMA((2 + blocks,)),
        ],
        compiler_params=pltpu.CompilerParams(
            collective_id=0, has_side_effects=True, vmem_limit_bytes=56 * 1024 * 1024
        ),
        name="block",
    )(*args)
    square = jax.ShapeDtypeStruct((width, width), F32)
    return pl.pallas_call(
        finish_kernel,
        out_shape=(jax.ShapeDtypeStruct((fine, width), F32),) + (square,) * 6,
        in_specs=[anywhere] * 2,
        out_specs=(anywhere,) * 7,
        scratch_shapes=[
            pltpu.VMEM((fine, width), F32),
            pltpu.VMEM((6 * width, width), F32),
            pltpu.SemaphoreType.DMA((6 + CUTS,)),
            pltpu.SemaphoreType.DMA((6 + CUTS,)),
        ],
        compiler_params=pltpu.CompilerParams(vmem_limit_bytes=56 * 1024 * 1024),
        name="finish",
    )(node_grad, sums)


def solution(mesh):
    rows = P(("grp", "dom"), None)
    flat = P(("grp", "dom"))
    whole = P()
    in_specs = (rows,) * 3 + (whole,) * 6 + (rows, flat, rows, rows, flat, rows)
    out_specs = (rows,) + (whole,) * 6
    return jax.shard_map(
        functools.partial(body, mesh.shape["grp"], mesh.shape["dom"]),
        mesh=mesh,
        in_specs=in_specs,
        out_specs=out_specs,
        check_vma=False,
    )
```
